128 devices in a mesh: seq: 4 (over z), shard: 8 (over x, core), grp: 4 (over y).
Axes of the slice: x: 4, y: 4, z: 4, core: 2. Of those that a mesh axis runs over, the one named last changes fastest.
Arguments:
- tokens: bfloat16 [4, 8, 512, 2048], P('grp', 'shard', 'seq'), may hold values from -6 to 6
- seq_lengths: int32 [4, 6], P('grp'), may hold values from 1 to 2048, 4096 in all within a row
- seq_order: int32 [4, 6], P('grp'), may hold values from 0 to 5, each once within a row
- norm_gain: bfloat16 [2048], P(('seq', 'shard')), may hold values from 0.5 to 1.5
- query_weight: bfloat16 [2048, 2048], P(('seq', 'shard')), may hold values from -0.125 to 0.125
- key_value_weight: bfloat16 [2048, 256], P(('seq', 'shard')), may hold values from -0.125 to 0.125
- out_weight: bfloat16 [2048, 2048], P(('seq', 'shard')), may hold values from -1 to 1
- mlp_gain: bfloat16 [2048], P(('seq', 'shard')), may hold values from 0.5 to 1.5
- gate_weight: bfloat16 [2048, 6144], P(('seq', 'shard')), may hold values from -0.125 to 0.125
- up_weight: bfloat16 [2048, 6144], P(('seq', 'shard')), may hold values from -0.125 to 0.125
- down_weight: bfloat16 [6144, 2048], P(('seq', 'shard')), may hold values from -0.078125 to 0.078125
- cotangent: bfloat16 [4, 8, 512, 2048], P('grp', 'shard', 'seq'), may hold values from -6 to 6
Outputs:
- layer_output: bfloat16 [4, 8, 512, 2048], P('grp', 'shard', 'seq')
- input_grad: float32 [4, 8, 512, 2048], P('grp', 'shard', 'seq')
- norm_gain_grad: float32 [2048], P(('seq', 'shard'))
- query_weight_grad: float32 [2048, 2048], P(('seq', 'shard'))
- key_value_weight_grad: float32 [2048, 256], P(('seq', 'shard'))
- out_weight_grad: float32 [2048, 2048], P(('seq', 'shard'))
- mlp_gain_grad: float32 [2048], P(('seq', 'shard'))
- gate_weight_grad: float32 [2048, 6144], P(('seq', 'shard'))
- up_weight_grad: float32 [2048, 6144], P(('seq', 'shard'))
- down_weight_grad: float32 [6144, 2048], P(('seq', 'shard'))
The draws below stay inside these ranges and needn't reach their ends.
All inputs are finite; a program needn't handle non-finite values.
Results may differ from the reference program's by a relative error of at most 0.028.
Values may be sent and summed in bfloat16 or wider, within the bound.
No kernel may reach another device: no remote copies, remote signals or barrier semaphores. Data moves between devices by JAX's collectives and lax.ppermute only.
A program may use at most 320 MiB of HBM per device.

```python
import math
import jax
import jax.numpy as jnp
import numpy as np
from jax import lax

D = 2048
HEADS = 16
HD = 128
FF = 6144
WINDOW = 1024
NSEQ = 6
GROUP_TOK = 512
POOL = 4096
MAXLEN = 2048
N_SHARD = 8
N_GRP = 4


def block_levels(rng, extent, shards, low, largest):
    def one(dim, shards_of):
        steps = jax.random.uniform(jax.random.fold_in(jax.random.fold_in(rng, 6), dim), (shards_of,), jnp.float32, low / len(shards), largest / len(shards))
        return jnp.repeat(jnp.exp(steps), extent[dim] // shards_of).reshape((-1,) + (1,) * (len(extent) - dim - 1))

    factor_of = one(*shards[0])
    for cut in shards[1:]:
        factor_of = factor_of * one(*cut)
    return factor_of


def length_profile(number_of, total, most, lean):
    weights = [(1 << 20) // math.isqrt(standing ** lean) + 1 for standing in range(2, number_of + 1)]
    rest, counts = total - most - (number_of - 1), [1] * (number_of - 1)
    while rest > 0:
        candidates = [i for i in range(number_of - 1) if counts[i] < most]
        whole, budget = sum([weights[i] for i in candidates]), rest
        for i in candidates:
            extra = min(most - counts[i], max(1, budget * weights[i] // whole), rest)
            counts[i] = counts[i] + extra
            rest = rest - extra
    return np.array([most] + counts)


def ragged(stream_key, count, total, limit, lean):
    if count == 2:
        one = jax.random.randint(stream_key, (), max(1, total - limit), min(limit, total - 1) + 1)
        return jnp.stack([one, total - one])
    sizes = jnp.asarray(length_profile(count, total, limit, lean), jnp.int32)
    twos = (count - 1) // 2
    giver, sink = sizes[1:1 + 2 * twos:2], sizes[2:2 + 2 * twos:2]
    room = jnp.minimum(giver - 1, limit - sink)
    moved = jax.random.randint(jax.random.fold_in(stream_key, 1), (twos,), 0, 1 << 20) % (room + 1)
    sizes = sizes.at[1:1 + 2 * twos:2].set(giver - moved).at[2:2 + 2 * twos:2].set(sink + moved)
    return sizes[jax.random.permutation(jax.random.fold_in(stream_key, 2), count)]


def scatter_about(stream_key, dims, scale, most, split=(), held_as=jnp.bfloat16):
    loudness = block_levels(stream_key, dims, split, -0.22, 0.18) if split else 1.0
    values = jax.random.normal(stream_key, dims, jnp.float32) * scale * loudness
    return jnp.minimum(jnp.maximum(values, -most), most).astype(held_as)


def setup_inputs(seed: int = 0) -> dict:
    splits = jax.random.split(jax.random.key(seed), 13)
    return {
        "tokens": scatter_about(splits[0], (N_GRP, N_SHARD, GROUP_TOK, D), 1.0, 6.0, ((0, 4), (1, 8), (2, 4))),
        "seq_lengths": jax.vmap(lambda own: ragged(own, NSEQ, POOL, MAXLEN, 2))(jax.random.split(splits[1], N_GRP)).reshape((N_GRP, NSEQ)).astype(jnp.int32),
        "seq_order": jax.vmap(lambda own: jax.random.permutation(own, NSEQ))(jax.random.split(splits[2], N_GRP)).reshape((N_GRP, NSEQ)).astype(jnp.int32),
        "norm_gain": jnp.clip(1.0 + 0.1 * jax.random.normal(splits[3], (D,), jnp.float32), 0.5, 1.5).astype(jnp.bfloat16),
        "query_weight": scatter_about(splits[4], (D, D), D ** -0.5, 0.125, ((0, 32),)),
        "key_value_weight": scatter_about(splits[5], (D, 2 * HD), D ** -0.5, 0.125, ((0, 32),)),
        "out_weight": scatter_about(splits[6], (D, D), (D // 64) ** -0.5, 1.0, ((0, 32),)),
        "mlp_gain": jnp.clip(1.0 + 0.1 * jax.random.normal(splits[7], (D,), jnp.float32), 0.5, 1.5).astype(jnp.bfloat16),
        "gate_weight": scatter_about(splits[8], (D, FF), D ** -0.5, 0.125, ((0, 32),)),
        "up_weight": scatter_about(splits[9], (D, FF), D ** -0.5, 0.125, ((0, 32),)),
        "down_weight": scatter_about(splits[10], (FF, D), FF ** -0.5, 0.078125, ((0, 32),)),
        "cotangent": scatter_about(splits[11], (N_GRP, N_SHARD, GROUP_TOK, D), 1.0, 6.0, ((0, 4), (1, 8), (2, 4))),
    }


@jax.custom_vjp
def low(v):
    return lax.optimization_barrier(v.astype(jnp.bfloat16)).astype(jnp.float32)

@jax.custom_vjp
def low_back(v):
    return v

def low_keep(v):
    return (low(v), None)

def low_pass(kept, grad):
    return (grad,)

def back_keep(v):
    return (v, None)

def back_low(kept, grad):
    return (low(grad),)
low.defvjp(low_keep, low_pass)
low_back.defvjp(back_keep, back_low)
highest = lax.Precision.HIGHEST
epsilon = 1e-06
big_negative = -1e+30

def rms_scale(values, gain):
    return values * lax.rsqrt(lax.optimization_barrier(jnp.mean(values * values, axis=-1, keepdims=True)) + epsilon) * gain

def rotate(values, place, sign):
    half_width = values.shape[-1] // 2
    frequency = 10000.0 ** (-jnp.arange(half_width, dtype=jnp.float32) / half_width)
    angle = place.astype(jnp.float32)[..., None] * frequency
    cosine = jnp.cos(angle)
    sine = sign * jnp.sin(angle)
    first = values[..., :half_width]
    second = values[..., half_width:]
    return jnp.concatenate([first * cosine - second * sine, first * sine + second * cosine], axis=-1)

def layout(lengths, packing, positions):
    slots = jnp.arange(lengths.shape[0], dtype=jnp.int32)
    picked = (packing[:, None] == slots[None, :]).astype(jnp.int32)
    packed = lax.optimization_barrier(jnp.sum(picked * lengths[None, :], axis=1, dtype=jnp.int32))
    ends = jnp.cumsum(packed, dtype=jnp.int32)
    starts = ends - packed
    segment = lax.optimization_barrier(jnp.sum((positions[:, None] >= ends[None, :]).astype(jnp.int32), axis=1, dtype=jnp.int32))
    begin = lax.optimization_barrier(jnp.sum(jnp.where(segment[:, None] == slots[None, :], starts[None, :], 0), axis=1, dtype=jnp.int32))
    segment = jnp.where(positions < 0, -1, segment)
    return (segment, positions - begin)

def reference(tokens, seq_lengths, seq_order, norm_gain, query_weight, key_value_weight, out_weight, mlp_gain, gate_weight, up_weight, down_weight, cotangent):
    block_rows = min(GROUP_TOK, 1024)
    block_count = POOL // block_rows
    span_rows = block_rows + WINDOW
    score_scale = HD ** (-0.5)
    query_index = jnp.arange(POOL, dtype=jnp.int32)
    key_index = jnp.arange(POOL + WINDOW, dtype=jnp.int32) - WINDOW
    query_segment, query_place = jax.vmap(layout, in_axes=(0, 0, None))(seq_lengths, seq_order, query_index)
    key_segment, key_place = jax.vmap(layout, in_axes=(0, 0, None))(seq_lengths, seq_order, key_index)

    def forward(inputs, gain_one, w_query, w_pair, w_out, gain_two, w_gate, w_upper, w_down):
        normed_one = low(rms_scale(inputs, gain_one))
        query_pre = low_back(jnp.einsum('gtd,de->gte', normed_one, w_query, precision=highest))
        queries = low(rotate(query_pre.reshape(N_GRP, POOL, HEADS, HD), query_place[..., None], 1.0))
        pair_pre = jnp.einsum('gtd,de->gte', normed_one, w_pair, precision=highest)
        keys_pre = low_back(pair_pre[..., :HD])
        keys = low(rotate(keys_pre, query_place, 1.0))
        values = low(low_back(pair_pre[..., HD:]))
        padding = jnp.zeros((N_GRP, WINDOW, HD), jnp.float32)
        keys = jnp.concatenate([padding, keys], axis=1)
        values = jnp.concatenate([padding, values], axis=1)

        def attend(number):
            start = number * block_rows
            query_block = lax.dynamic_slice_in_dim(queries, start, block_rows, 1)
            key_block = lax.dynamic_slice_in_dim(keys, start, span_rows, 1)
            value_block = lax.dynamic_slice_in_dim(values, start, span_rows, 1)
            query_seg = lax.dynamic_slice_in_dim(query_segment, start, block_rows, 1)
            key_seg = lax.dynamic_slice_in_dim(key_segment, start, span_rows, 1)
            query_pos = start + jnp.arange(block_rows, dtype=jnp.int32)
            key_pos = start - WINDOW + jnp.arange(span_rows, dtype=jnp.int32)
            raw = jnp.einsum('gqhd,gkd->ghqk', query_block, key_block, precision=highest)
            scores = low_back(raw * score_scale)
            distance = query_pos[:, None] - key_pos[None, :]
            allowed = (query_seg[:, :, None] == key_seg[:, None, :]) & ((distance >= 0) & (distance < WINDOW))[None]
            scores = jnp.where(allowed[:, None], scores, big_negative)
            top_score = lax.optimization_barrier(jnp.max(scores, axis=-1, keepdims=True))
            expo = jnp.exp(scores - top_score)
            soft = low(expo / lax.optimization_barrier(jnp.sum(expo, axis=-1, keepdims=True)))
            return jnp.einsum('ghqk,gkd->gqhd', soft, value_block, precision=highest)
        blocks = lax.map(jax.checkpoint(attend), jnp.arange(block_count, dtype=jnp.int32))
        attended = jnp.moveaxis(blocks, 0, 1).reshape(N_GRP, POOL, D)
        attended = low(low_back(attended))
        branch = low_back(jnp.einsum('gtd,de->gte', attended, w_out, precision=highest))
        middle = inputs + branch
        normed_two = low(rms_scale(middle, gain_two))
        gate_values = low_back(jnp.einsum('gtd,df->gtf', normed_two, w_gate, precision=highest))
        upper_values = low_back(jnp.einsum('gtd,df->gtf', normed_two, w_upper, precision=highest))
        hidden = low(jax.nn.gelu(gate_values) * upper_values)
        return middle + low_back(jnp.einsum('gtf,fd->gtd', hidden, w_down, precision=highest))
    floats = (tokens.reshape(N_GRP, POOL, D).astype(jnp.float32), norm_gain.astype(jnp.float32), query_weight.astype(jnp.float32), key_value_weight.astype(jnp.float32), out_weight.astype(jnp.float32), mlp_gain.astype(jnp.float32), gate_weight.astype(jnp.float32), up_weight.astype(jnp.float32), down_weight.astype(jnp.float32))
    result, pullback = jax.vjp(forward, *floats)
    grads = pullback(cotangent.reshape(N_GRP, POOL, D).astype(jnp.float32))
    shaped = (N_GRP, N_SHARD, GROUP_TOK, D)
    return (result.astype(jnp.bfloat16).reshape(shaped), grads[0].reshape(shaped), grads[1], grads[2], grads[3], grads[4], grads[5], grads[6], grads[7], grads[8])
```

```python
import functools

import jax
import jax.numpy as jnp
from jax import lax
from jax.experimental import pallas as pl
from jax.experimental.pallas import tpu as pltpu
from jax.sharding import PartitionSpec as P

HEADS = 16
HD = 128
WINDOW = 1024
RING = 4
BLOCK = 128
CHUNK = 32
FBLOCK = 512

epsilon = 1e-06
big_negative = -1e30


def send(value, axis, steps):
    count = lax.axis_size(axis)
    return lax.ppermute(value, axis, [(i, (i + steps) % count) for i in range(count)])


def send_x(value, steps):
    return lax.ppermute(
        value,
        "shard",
        [(x * 2 + c, (x + steps) % RING * 2 + c) for x in range(RING) for c in range(2)],
    )


def send_core(value):
    return lax.ppermute(
        value, "shard", [(x * 2 + c, x * 2 + 1 - c) for x in range(RING) for c in range(2)]
    )


def fence(*values):
    return lax.optimization_barrier(values)


def shifted(value, axis, steps):
    count = lax.axis_size(axis)
    initial, last = (max(0, -steps), min(count, count - steps))
    return lax.ppermute(value, axis, [(i, i + steps) for i in range(initial, last)])


def gather_ring(piece, axis):
    half = piece.shape[0] // 2
    after = send(piece, axis, -1)
    before = send(piece, axis, 1)
    far_a = send(after[:half], axis, -1)
    far_b = send(before[half:], axis, 1)
    return [piece, after, jnp.concatenate([far_a, far_b], axis=0), before]


def scatter_ring(parts, axis):
    own, nxt, far, prv = parts
    half = own.shape[0] // 2
    got_a = send(far[:half].astype(jnp.bfloat16), axis, 1).astype(jnp.float32)
    got_b = send(far[half:].astype(jnp.bfloat16), axis, -1).astype(jnp.float32)
    nxt = jnp.concatenate([nxt[:half] + got_a, nxt[half:]], axis=0)
    prv = jnp.concatenate([prv[:half], prv[half:] + got_b], axis=0)
    from_prv = send(nxt.astype(jnp.bfloat16), axis, 1).astype(jnp.float32)
    from_nxt = send(prv.astype(jnp.bfloat16), axis, -1).astype(jnp.float32)
    return own + from_prv + from_nxt


def scatter_direct(pick, axis, index):
    got = [send(pick((index + k) % RING).astype(jnp.bfloat16), axis, k) for k in range(1, RING)]
    return pick(index) + sum(one.astype(jnp.float32) for one in got)


def gather_direct(piece, axis, index):
    got = [send(piece, axis, -k) for k in range(1, RING)]
    return ordered([piece] + got, index)


def scatter_x(pick, index):
    parts = [pick((index + k) % RING) for k in range(RING)]
    got = [send_x(parts[k].astype(jnp.bfloat16), k) for k in range(1, RING)]
    return parts[0] + sum(one.astype(jnp.float32) for one in got)


def ordered(parts, index):
    twice = jnp.stack(parts + parts, axis=0)
    return lax.dynamic_slice_in_dim(twice, (RING - index) % RING, RING, 0)


def exchange_parts(pick, axis, index):
    got = [pick((index + k) % RING) for k in range(RING)]
    return [got[0]] + [send(got[k], axis, k) for k in range(1, RING)]


def by_source(got, index):
    return ordered([got[0], got[3], got[2], got[1]], index)


def exchange(pick, axis, index):
    return by_source(exchange_parts(pick, axis, index), index)


def row_blocks(total):
    rows = total.shape[0] // RING
    return [total[i * rows : (i + 1) * rows] for i in range(RING)]


def norm_scale(values):
    return lax.rsqrt(jnp.mean(values * values, axis=-1, keepdims=True) + epsilon)


def norm_back(values, scale, gain, grad):
    scaled = grad * gain
    dot = jnp.mean(scaled * values, axis=-1, keepdims=True)
    return scaled * scale - values * (scale * scale * scale * dot)


def slot_starts(lengths, packing):
    slots = jnp.arange(lengths.shape[0], dtype=jnp.int32)
    picked = (packing[:, None] == slots[None, :]).astype(jnp.int32)
    packed = jnp.sum(picked * lengths[None, :], axis=1, dtype=jnp.int32)
    return jnp.cumsum(packed, dtype=jnp.int32) - packed


def rotation(place):
    half_width = HD // 2
    frequency = 10000.0 ** (-jnp.arange(half_width, dtype=jnp.float32) / half_width)
    angle = place.astype(jnp.float32)[:, None] * frequency
    cosine, sine = jnp.cos(angle), jnp.sin(angle)
    return jnp.concatenate([cosine, cosine], axis=1), jnp.concatenate([-sine, sine], axis=1)


def matmul(left, right):
    return jnp.dot(left, right, preferred_element_type=jnp.float32)


def inner_rows(left, right):
    return lax.dot_general(
        left, right, (((0,), (0,)), ((), ())), preferred_element_type=jnp.float32
    )


def inner_cols(left, right):
    return lax.dot_general(
        left, right, (((1,), (1,)), ((), ())), preferred_element_type=jnp.float32
    )


def tile_mask(info, tile, first_row, rows, reach, group):
    shard, seq = info[0], info[1]
    base = shard * group
    row = lax.broadcasted_iota(jnp.int32, (rows, 1), 0) + first_row
    query = base + (seq + tile) % RING * BLOCK + row
    begin = jnp.zeros_like(query)
    for slot in range(info.shape[0] - 2):
        start = info[2 + slot]
        begin = jnp.where(query >= start, jnp.maximum(begin, start), begin)
    lowest = jnp.maximum(begin, query - (WINDOW - 1))
    lane = lax.broadcasted_iota(jnp.int32, (1, reach), 1)
    block = lane // group
    in_block = lane - block * group
    key = base + (block - (reach // group - 1)) * group
    key = key + (seq + in_block // BLOCK) % RING * BLOCK + in_block % BLOCK
    return (key <= query) & (key >= lowest)


def attend_kernel(info, q_ref, *refs, heads, group):
    kv_refs, (out_ref, lse_ref, scores_ref, soft_ref) = refs[:-4], refs[-4:]
    reach = group * len(kv_refs)
    tile = pl.program_id(0)
    q = jnp.concatenate([q_ref[:, h * HD : (h + 1) * HD] for h in range(heads)], axis=0)
    for b, kv in enumerate(kv_refs):
        scores_ref[:, b * group : (b + 1) * group] = inner_cols(q, kv[:, :HD])
    for part in range(BLOCK // CHUNK):
        mask = tile_mask(info, tile, part * CHUNK, CHUNK, reach, group)
        for h in range(heads):
            at = pl.ds(h * BLOCK + part * CHUNK, CHUNK)
            scores = jnp.where(mask, scores_ref[at, :] * (HD**-0.5), big_negative)
            top = jnp.max(scores, axis=1, keepdims=True)
            expo = jnp.exp(scores - top)
            total = jnp.sum(expo, axis=1, keepdims=True)
            soft_ref[at, :] = (expo * (1.0 / total)).astype(jnp.bfloat16)
            lse_ref[0, at, :] = jnp.broadcast_to(top + jnp.log(total), (CHUNK, HD))
    acc = None
    for b, kv in enumerate(kv_refs):
        term = jnp.dot(soft_ref[:, b * group : (b + 1) * group], kv[:, HD:], preferred_element_type=jnp.float32)
        acc = term if acc is None else acc + term
    for h in range(heads):
        out_ref[:, h * HD : (h + 1) * HD] = acc[h * BLOCK : (h + 1) * BLOCK].astype(jnp.bfloat16)


def attend(info, queries, kvs):
    group, width = queries.shape
    heads = width // HD
    reach = group * len(kvs)
    whole = pl.BlockSpec((group, 2 * HD), lambda i: (0, 0))
    rows = pl.BlockSpec((BLOCK, width), lambda i: (i, 0))
    return pl.pallas_call(
        functools.partial(attend_kernel, heads=heads, group=group),
        grid=(group // BLOCK,),
        in_specs=[pl.BlockSpec(memory_space=pltpu.SMEM), rows] + [whole] * len(kvs),
        out_specs=[rows, pl.BlockSpec((1, heads * BLOCK, HD), lambda i: (i, 0, 0))],
        out_shape=[
            jax.ShapeDtypeStruct((group, width), jnp.bfloat16),
            jax.ShapeDtypeStruct((group // BLOCK, heads * BLOCK, HD), jnp.float32),
        ],
        scratch_shapes=[
            pltpu.VMEM((heads * BLOCK, reach), jnp.float32),
            pltpu.VMEM((heads * BLOCK, reach), jnp.bfloat16),
        ],
        compiler_params=pltpu.CompilerParams(vmem_limit_bytes=40 * 1024 * 1024),
        name="attend",
    )(info, queries, *kvs)


def attend_back_kernel(info, q_ref, do_ref, lse_ref, cos_ref, sin_ref, *refs, heads, group):
    count = len(refs) - 6
    kv_refs, (dq_ref, dkv_ref, scores_ref, dsoft_ref, soft_ref, dscores_ref) = refs[:count], refs[count:]
    reach = group * count
    tile = pl.program_id(0)

    @pl.when(tile == 0)
    def _():
        dkv_ref[...] = jnp.zeros_like(dkv_ref)

    q = jnp.concatenate([q_ref[:, h * HD : (h + 1) * HD] for h in range(heads)], axis=0)
    do = jnp.concatenate([do_ref[:, h * HD : (h + 1) * HD] for h in range(heads)], axis=0)
    for b, kv in enumerate(kv_refs):
        at = slice(b * group, (b + 1) * group)
        scores_ref[:, at] = inner_cols(q, kv[:, :HD])
        dsoft_ref[:, at] = inner_cols(do, kv[:, HD:])
    for part in range(BLOCK // CHUNK):
        mask = tile_mask(info, tile, part * CHUNK, CHUNK, reach, group)
        for h in range(heads):
            at = pl.ds(h * BLOCK + part * CHUNK, CHUNK)
            lse = lse_ref[0, at, 0:1]
            scores = jnp.where(mask, scores_ref[at, :] * (HD**-0.5), big_negative)
            soft = jnp.exp(scores - lse)
            dsoft = dsoft_ref[at, :]
            delta = jnp.sum(soft * dsoft, axis=1, keepdims=True)
            soft_ref[at, :] = soft.astype(jnp.bfloat16)
            dscores_ref[at, :] = (soft * (dsoft - delta)).astype(jnp.bfloat16)
    dq = None
    for b, kv in enumerate(kv_refs):
        at = slice(b * group, (b + 1) * group)
        term = jnp.dot(dscores_ref[:, at], kv[:, :HD], preferred_element_type=jnp.float32)
        dq = term if dq is None else dq + term
        dkv_ref[b, :, :HD] += inner_rows(dscores_ref[:, at], q) * (HD**-0.5)
        dkv_ref[b, :, HD:] += inner_rows(soft_ref[:, at], do)
    cos, sin = cos_ref[...], sin_ref[...]
    for h in range(heads):
        one = dq[h * BLOCK : (h + 1) * BLOCK] * (HD**-0.5)
        one = one * cos - pltpu.roll(one, HD // 2, 1) * sin
        dq_ref[:, h * HD : (h + 1) * HD] = one.astype(jnp.bfloat16)


def attend_back(info, queries, grads, lse, cos, sin, kvs):
    group, width = queries.shape
    heads = width // HD
    reach = group * len(kvs)
    whole = pl.BlockSpec((group, 2 * HD), lambda i: (0, 0))
    rows = pl.BlockSpec((BLOCK, width), lambda i: (i, 0))
    table = pl.BlockSpec((BLOCK, HD), lambda i: (i, 0))
    return pl.pallas_call(
        functools.partial(attend_back_kernel, heads=heads, group=group),
        grid=(group // BLOCK,),
        in_specs=[
            pl.BlockSpec(memory_space=pltpu.SMEM),
            rows,
            rows,
            pl.BlockSpec((1, heads * BLOCK, HD), lambda i: (i, 0, 0)),
            table,
            table,
        ]
        + [whole] * len(kvs),
        out_specs=[rows, pl.BlockSpec((len(kvs), group, 2 * HD), lambda i: (0, 0, 0))],
        out_shape=[
            jax.ShapeDtypeStruct((group, width), jnp.bfloat16),
            jax.ShapeDtypeStruct((len(kvs), group, 2 * HD), jnp.float32),
        ],
        scratch_shapes=[
            pltpu.VMEM((heads * BLOCK, reach), jnp.float32),
            pltpu.VMEM((heads * BLOCK, reach), jnp.float32),
            pltpu.VMEM((heads * BLOCK, reach), jnp.bfloat16),
            pltpu.VMEM((heads * BLOCK, reach), jnp.bfloat16),
        ],
        compiler_params=pltpu.CompilerParams(vmem_limit_bytes=40 * 1024 * 1024),
        name="attend_back",
    )(info, queries, grads, lse, cos, sin, *kvs)


def project_kernel(
    info, tok_ref, cos_ref, sin_ref, own, after, far_a, far_b, before, near, far,
    n_ref, q_ref, kv_ref, gains_ref, w_ref, sems, *, heads, block
):
    q_cols = heads * HD

    @pl.when(pl.program_id(0) == 0)
    def _():
        x, core = info[0] // 2, info[0] % 2
        copies = []

        def fetch(piece, k, other, first):
            place = (x + k) % RING * 2 + (1 - core if other else core)
            for i in range(piece.shape[0]):
                at = pl.multiple_of((first + i) * 8 * block + place * block, block)
                copies.append(
                    pltpu.make_async_copy(
                        piece.at[i], w_ref.at[pl.ds(at, block), :], sems.at[len(copies)]
                    )
                )

        half = RING // 2
        fetch(own, 0, False, 0)
        fetch(after, 1, False, 0)
        fetch(far_a, 2, False, 0)
        fetch(far_b, 2, False, half)
        fetch(before, 3, False, 0)
        fetch(near.at[0], 0, True, 0)
        fetch(near.at[1], 1, True, 0)
        fetch(far, 2, True, 0)
        fetch(near.at[2], 3, True, 0)
        for copy in copies:
            copy.start()
        for copy in copies:
            copy.wait()
        pick = lax.broadcasted_iota(jnp.int32, (8, HD), 0) == lax.broadcasted_iota(
            jnp.int32, (8, HD), 1
        )
        gains_ref[...] = inner_cols(pick.astype(jnp.bfloat16), w_ref[:, q_cols + 2 * HD :])

    x = tok_ref[...].astype(jnp.float32)
    scale = lax.rsqrt(jnp.mean(x * x, axis=1, keepdims=True) + epsilon)
    normed = (x * scale * gains_ref[0:1, :]).astype(jnp.bfloat16)
    n_ref[...] = normed
    qkv = jnp.dot(normed, w_ref[:, : q_cols + 2 * HD], preferred_element_type=jnp.float32)
    cos, sin = cos_ref[...], sin_ref[...]
    for h in range(heads + 1):
        one = qkv[:, h * HD : (h + 1) * HD]
        one = (one * cos + pltpu.roll(one, HD // 2, 1) * sin).astype(jnp.bfloat16)
        if h < heads:
            q_ref[:, h * HD : (h + 1) * HD] = one
        else:
            kv_ref[:, :HD] = one
    kv_ref[:, HD:] = qkv[:, (heads + 1) * HD :].astype(jnp.bfloat16)


def project(info, tokens, cos, sin, pieces):
    group, width = tokens.shape
    block, columns = pieces[0].shape[1:]
    heads = columns // HD - 3
    rows = lambda n: pl.BlockSpec((BLOCK, n), lambda i: (i, 0))
    whole = lambda shape: pl.BlockSpec(shape, lambda i: (0, 0))
    return pl.pallas_call(
        functools.partial(project_kernel, heads=heads, block=block),
        grid=(group // BLOCK,),
        in_specs=[pl.BlockSpec(memory_space=pltpu.SMEM), rows(width), rows(HD), rows(HD)]
        + [pl.BlockSpec(memory_space=pl.ANY)] * len(pieces),
        out_specs=[
            rows(width),
            rows(heads * HD),
            rows(2 * HD),
            whole((8, width)),
            whole((width, columns)),
        ],
        out_shape=[
            jax.ShapeDtypeStruct((group, width), jnp.bfloat16),
            jax.ShapeDtypeStruct((group, heads * HD), jnp.bfloat16),
            jax.ShapeDtypeStruct((group, 2 * HD), jnp.bfloat16),
            jax.ShapeDtypeStruct((8, width), jnp.float32),
            jax.ShapeDtypeStruct((width, columns), jnp.bfloat16),
        ],
        scratch_shapes=[pltpu.SemaphoreType.DMA((8 * RING,))],
        compiler_params=pltpu.CompilerParams(vmem_limit_bytes=40 * 1024 * 1024),
        name="project",
    )(info, tokens, cos, sin, *pieces)


def feed_kernel(n_ref, gh_ref, gate_ref, up_ref, hidden_ref, grad_ref, back_ref):
    step = pl.program_id(0)
    size = gate_ref.shape[1]
    inner = grad_ref.shape[1] // 2
    gate = jnp.dot(n_ref[...], gate_ref[...], preferred_element_type=jnp.float32)
    upper = jnp.dot(n_ref[...], up_ref[...], preferred_element_type=jnp.float32)
    grad_hidden = gh_ref[...]
    root, cube = 0.7978845608028654, 0.044715
    square = gate * gate
    bend = jnp.tanh(root * gate * (1.0 + cube * square))
    half = 0.5 * (1.0 + bend)
    act = gate * half
    slope = half + 0.5 * gate * (1.0 - bend * bend) * (root * (1.0 + 3.0 * cube * square))
    hidden_ref[...] = (act * upper).astype(jnp.bfloat16)
    grad_gate = (grad_hidden * upper * slope).astype(jnp.bfloat16)
    grad_upper = (grad_hidden * act).astype(jnp.bfloat16)
    grad_ref[:, pl.ds(pl.multiple_of(step * size, size), size)] = grad_gate
    grad_ref[:, pl.ds(pl.multiple_of(inner + step * size, size), size)] = grad_upper
    back = inner_cols(grad_gate, gate_ref[...]) + inner_cols(grad_upper, up_ref[...])

    @pl.when(step == 0)
    def _():
        back_ref[...] = back

    @pl.when(step > 0)
    def _():
        back_ref[...] += back


def feed(normed, grad_hidden, weights):
    group, width = normed.shape
    inner = grad_hidden.shape[1]
    steps = inner // FBLOCK
    whole = lambda n: pl.BlockSpec((group, n), lambda i: (0, 0))
    columns = pl.BlockSpec((group, FBLOCK), lambda i: (0, i))
    return pl.pallas_call(
        feed_kernel,
        grid=(steps,),
        in_specs=[
            whole(width),
            columns,
            pl.BlockSpec((width, FBLOCK), lambda i: (0, i)),
            pl.BlockSpec((width, FBLOCK), lambda i: (0, steps + i)),
        ],
        out_specs=[columns, whole(2 * inner), whole(width)],
        out_shape=[
            jax.ShapeDtypeStruct((group, inner), jnp.bfloat16),
            jax.ShapeDtypeStruct((group, 2 * inner), jnp.bfloat16),
            jax.ShapeDtypeStruct((group, width), jnp.float32),
        ],
        compiler_params=pltpu.CompilerParams(vmem_limit_bytes=56 * 1024 * 1024),
        cost_estimate=pl.CostEstimate(
            flops=8 * group * width * inner,
            bytes_accessed=4 * width * inner,
            transcendentals=group * inner,
        ),
        name="feed",
    )(normed, grad_hidden, weights, weights)


def shards(
    tokens,
    seq_lengths,
    seq_order,
    norm_gain,
    query_weight,
    key_value_weight,
    out_weight,
    mlp_gain,
    gate_weight,
    up_weight,
    down_weight,
    cotangent,
):
    rows = tokens.shape[2]
    width = tokens.shape[3]
    group_rows = rows * RING
    q_cols = HEADS // RING * HD
    f_cols = gate_weight.shape[1] // RING
    own_rows = query_weight.shape[0]
    shard_index = lax.axis_index("shard")
    seq_index = lax.axis_index("seq")
    grp_index = lax.axis_index("grp")
    own_tokens = tokens[0, 0]
    own_cotangent = cotangent[0, 0]

    gains = jnp.pad(jnp.stack([norm_gain, mlp_gain], axis=1), ((0, 0), (0, HD - 2)))

    def pick_q(i):
        own = lax.dynamic_slice_in_dim(query_weight, i * q_cols, q_cols, 1)
        return jnp.concatenate([own, key_value_weight, gains], axis=1)

    def pick_f(i):
        return jnp.concatenate(
            [
                lax.dynamic_slice_in_dim(gate_weight, i * f_cols, f_cols, 1),
                lax.dynamic_slice_in_dim(up_weight, i * f_cols, f_cols, 1),
            ],
            axis=1,
        )

    group_start = shard_index * group_rows
    ring_rows = (seq_index + jnp.arange(RING, dtype=jnp.int32)) % RING * rows
    in_group = (ring_rows[:, None] + jnp.arange(rows, dtype=jnp.int32)[None, :]).reshape(-1)
    query_index = group_start + in_group
    starts = slot_starts(seq_lengths[0], seq_order[0])
    begins = jnp.max(
        jnp.where(query_index[:, None] >= starts[None, :], starts[None, :], 0), axis=1
    )
    cos, sin = rotation(query_index - begins)
    info = jnp.concatenate([jnp.stack([shard_index, seq_index]).astype(jnp.int32), starts])

    def scattered(grad, dim):
        return lax.psum_scatter(grad, "shard", scatter_dimension=dim, tiled=True)

    w_out = lax.all_gather(out_weight, "shard", axis=0, tiled=True)
    got = exchange_parts(pick_q, "seq", seq_index)
    tok_after = send(own_tokens, "seq", -1)
    tok_before = send(own_tokens, "seq", 1)
    *got, tok_after, tok_before, gate_weight, up_weight, down_weight = fence(
        *got, tok_after, tok_before, gate_weight, up_weight, down_weight
    )
    w_down = lax.all_gather(down_weight, "shard", axis=0, tiled=True)
    block = by_source(got, seq_index)
    block_after = send_x(block, -1)
    block_before = send_x(block, 1)
    half = rows // 2
    tok_far_a = send(tok_after[:half], "seq", -1)
    tok_far_b = send(tok_before[half:], "seq", 1)
    block_after, block_before, tok_far_a, tok_far_b, gate_weight, up_weight, w_out = fence(
        block_after, block_before, tok_far_a, tok_far_b, gate_weight, up_weight, w_out
    )
    block_far_a = send_x(block_after[: RING // 2], -1)
    block_far_b = send_x(block_before[RING // 2 :], 1)
    near = send_core(jnp.stack([block, block_after, block_before]))
    got = exchange_parts(pick_f, "seq", seq_index)
    block_far_a, block_far_b, near = fence(block_far_a, block_far_b, near)
    far = send_core(jnp.concatenate([block_far_a, block_far_b]))
    tokens_bf = jnp.concatenate([own_tokens, tok_after, tok_far_a, tok_far_b, tok_before], axis=0)
    pieces = (block, block_after, block_far_a, block_far_b, block_before, near, far)
    normed_one, queries, pair, gain_rows, w_attn = project(info, tokens_bf, cos, sin, pieces)
    *got, own_cotangent, pair = fence(*got, own_cotangent, pair)
    w_ff = lax.all_gather(by_source(got, seq_index), "shard", axis=1, tiled=True)
    w_ff = w_ff.reshape(width, -1)
    gain_one, gain_two = gain_rows[0], gain_rows[1]
    w_qkv = w_attn[:, : q_cols + 2 * HD]
    cot_after = send(own_cotangent, "seq", -1)
    cot_before = send(own_cotangent, "seq", 1)
    kvs = [shifted(pair, "shard", 2), shifted(pair, "shard", 1), pair]
    attended, lse = attend(info, queries, kvs)
    attended, cot_after, cot_before, w_down = fence(attended, cot_after, cot_before, w_down)
    cot_far_a = send(cot_after[:half], "seq", -1)
    cot_far_b = send(cot_before[half:], "seq", 1)
    all_cotangent = jnp.concatenate(
        [own_cotangent, cot_after, cot_far_a, cot_far_b, cot_before], axis=0
    )

    branch = scatter_ring(row_blocks(matmul(attended, w_out)), "seq")
    middle = own_tokens.astype(jnp.float32) + branch
    scale_two = norm_scale(middle)
    normed_two = (middle * scale_two * gain_two).astype(jnp.bfloat16)
    normed_two = jnp.concatenate(gather_ring(normed_two, "seq"), axis=0)
    grad_hidden, normed_two = fence(inner_cols(all_cotangent, w_down), normed_two)
    hidden, grad_ff, partial_two = feed(normed_two, grad_hidden, w_ff)
    grad_wff = inner_rows(normed_two, grad_ff).astype(jnp.bfloat16)
    grad_down = inner_rows(hidden, all_cotangent).astype(jnp.bfloat16)
    share_ff = scattered(grad_wff.reshape(RING, -1, 2 * f_cols), 1)
    grad_normed_two = scatter_ring(row_blocks(partial_two), "seq")
    grad_normed_two, grad_wff, grad_down = fence(grad_normed_two, grad_wff, grad_down)

    x_index, core = shard_index // 2, shard_index % 2
    part = own_rows // RING
    grad_down = grad_down.reshape(RING, 2, RING, -1, width)
    down_other = send_core(lax.dynamic_index_in_dim(grad_down, 1 - core, 1, keepdims=False))
    grad_middle = own_cotangent.astype(jnp.float32) + norm_back(
        middle, scale_two, gain_two, grad_normed_two
    )
    gain_two_terms = (grad_normed_two * middle * scale_two).astype(jnp.bfloat16)
    own_branch = grad_middle.astype(jnp.bfloat16)
    gb_after = send(own_branch, "seq", -1)
    gb_before = send(own_branch, "seq", 1)
    gb_after, gb_before, down_other, grad_down = fence(gb_after, gb_before, down_other, grad_down)
    gb_far_a = send(gb_after[:half], "seq", -1)
    gb_far_b = send(gb_before[half:], "seq", 1)
    mine = lax.dynamic_index_in_dim(grad_down, core, 1, keepdims=False).astype(jnp.float32)
    mine = (mine + down_other.astype(jnp.float32)).astype(jnp.bfloat16)
    down_parts = [
        lax.dynamic_index_in_dim(mine, (grp_index + k) % RING, 1, keepdims=False)
        for k in range(RING)
    ]
    down_a = send(down_parts[2][: RING // 2], "grp", 1)
    down_b = send(down_parts[2][RING // 2 :], "grp", -1)
    gb_far_a, gb_far_b, down_a, down_b, *down_parts = fence(
        gb_far_a, gb_far_b, down_a, down_b, *down_parts
    )
    grad_branch = jnp.concatenate([own_branch, gb_after, gb_far_a, gb_far_b, gb_before], axis=0)
    grad_attended = inner_cols(grad_branch, w_out).astype(jnp.bfloat16)
    down_own, down_next, _, down_last = [one.astype(jnp.float32) for one in down_parts]
    down_next = jnp.concatenate(
        [down_next[: RING // 2] + down_a.astype(jnp.float32), down_next[RING // 2 :]], axis=0
    ).astype(jnp.bfloat16)
    down_last = jnp.concatenate(
        [down_last[: RING // 2], down_last[RING // 2 :] + down_b.astype(jnp.float32)], axis=0
    ).astype(jnp.bfloat16)
    down_next = send(down_next, "grp", 1)
    down_last = send(down_last, "grp", -1)

    grad_queries, grad_table = attend_back(info, queries, grad_attended, lse, cos, sin, kvs)
    grad_wout = inner_rows(attended, grad_branch).astype(jnp.bfloat16)
    grad_queries, grad_table, share_ff, down_next, down_last, grad_wout = fence(
        grad_queries, grad_table, share_ff, down_next, down_last, grad_wout
    )
    share_out = scattered(grad_wout, 0)
    returned_two = shifted(grad_table[0].astype(jnp.bfloat16), "shard", -2)
    returned_one = shifted(grad_table[1].astype(jnp.bfloat16), "shard", -1)
    down_own = down_own + down_next.astype(jnp.float32) + down_last.astype(jnp.float32)
    down_own = scatter_x(
        lambda i: lax.dynamic_index_in_dim(down_own, i, 0, keepdims=False), x_index
    ).astype(jnp.bfloat16)
    returned_one, returned_two, down_own, share_ff, hidden = fence(
        returned_one, returned_two, down_own, share_ff, hidden
    )
    grad_pair = (
        grad_table[2] + returned_one.astype(jnp.float32) + returned_two.astype(jnp.float32)
    )
    grad_keys = grad_pair[:, :HD]
    swapped = jnp.concatenate([grad_keys[:, HD // 2 :], grad_keys[:, : HD // 2]], axis=1)
    grad_keys = grad_keys * cos - swapped * sin
    grad_pair = jnp.concatenate([grad_keys, grad_pair[:, HD:]], axis=1).astype(jnp.bfloat16)
    grad_qkv = jnp.concatenate([grad_queries, grad_pair], axis=1)
    all_tokens = tokens_bf.astype(jnp.float32)
    scale_one = norm_scale(all_tokens)
    partial_one = inner_cols(grad_qkv, w_qkv)
    gain_one_terms = (partial_one * all_tokens * scale_one).astype(jnp.bfloat16)
    columns = jnp.arange(HD)[None, :]
    first_column = jnp.broadcast_to(columns == 0, (group_rows, HD)).astype(jnp.bfloat16)
    second_column = jnp.broadcast_to(columns == 1, (rows, HD)).astype(jnp.bfloat16)
    grad_gains = inner_rows(gain_one_terms, first_column) + inner_rows(
        gain_two_terms, second_column
    )
    grad_attn = jnp.concatenate(
        fence(inner_rows(normed_one, grad_qkv).astype(jnp.bfloat16), grad_gains.astype(jnp.bfloat16)),
        axis=1,
    )

    def spread(share):
        share = share.reshape(RING, RING, part, -1)
        summed = scatter_direct(
            lambda i: lax.dynamic_index_in_dim(share, i, 1, keepdims=False).astype(jnp.float32),
            "grp",
            grp_index,
        )
        return summed.astype(jnp.bfloat16)

    def placed(summed):
        return exchange(
            lambda i: lax.dynamic_index_in_dim(summed, i, 0, keepdims=False), "seq", seq_index
        )

    def side_by_side(columns):
        return columns.transpose(1, 0, 2).reshape(columns.shape[1], -1)

    own_one, next_one, far_one, last_one = row_blocks(partial_one)
    one_a = send(far_one[:half].astype(jnp.bfloat16), "seq", 1)
    one_b = send(far_one[half:].astype(jnp.bfloat16), "seq", -1)
    sum_ff = spread(share_ff)
    one_a, one_b, sum_ff, grad_attn, share_out = fence(one_a, one_b, sum_ff, grad_attn, share_out)
    share_attn = scattered(grad_attn.reshape(RING, -1, grad_attn.shape[1]), 1)
    next_one = jnp.concatenate([next_one[:half] + one_a.astype(jnp.float32), next_one[half:]], axis=0)
    last_one = jnp.concatenate([last_one[:half], last_one[half:] + one_b.astype(jnp.float32)], axis=0)
    from_last = send(next_one.astype(jnp.bfloat16), "seq", 1)
    from_next = send(last_one.astype(jnp.bfloat16), "seq", -1)
    ff_columns = placed(sum_ff)
    from_last, from_next, ff_columns = fence(from_last, from_next, ff_columns)
    grad_normed_one = own_one + from_last.astype(jnp.float32) + from_next.astype(jnp.float32)
    own_inputs = own_tokens.astype(jnp.float32)
    input_grad = grad_middle + norm_back(
        own_inputs, norm_scale(own_inputs), gain_one, grad_normed_one
    )
    ff_rows = jnp.concatenate(
        [
            side_by_side(ff_columns[:, :, :f_cols]),
            side_by_side(ff_columns[:, :, f_cols:]),
            down_own.reshape(part, -1),
        ],
        axis=1,
    )
    ff_after = send(ff_rows, "grp", -1)
    ff_before = send(ff_rows, "grp", 1)
    ff_after, ff_before, share_attn, input_grad = fence(ff_after, ff_before, share_attn, input_grad)
    ff_far_a = send(ff_after[: part // 2], "grp", -1)
    ff_far_b = send(ff_before[part // 2 :], "grp", 1)

    from_out = share_out.reshape(RING, part, RING, -1).transpose(2, 0, 1, 3)
    from_out = from_out.reshape(RING, own_rows, -1)
    summed = spread(jnp.concatenate([share_attn, from_out], axis=2))
    ff_far = jnp.concatenate([ff_far_a, ff_far_b], axis=0)
    summed, ff_far = fence(summed, ff_far)
    ff_rows = ordered([ff_rows, ff_after, ff_far, ff_before], grp_index)
    ff_rows = ff_rows.reshape(own_rows, -1).astype(jnp.float32)
    share_gate = ff_rows[:, : RING * f_cols]
    share_upper = ff_rows[:, RING * f_cols : 2 * RING * f_cols]
    share_down = ff_rows[:, 2 * RING * f_cols :].reshape(-1, width)
    n_attn = share_attn.shape[2]
    out_own = side_by_side(summed[:, :, n_attn:])
    columns = placed(summed[:, :, :n_attn])
    summed = jnp.sum(columns[:, :, q_cols:].astype(jnp.float32), axis=0).astype(jnp.bfloat16)
    attn_rows = jnp.concatenate([side_by_side(columns[:, :, :q_cols]), out_own, summed], axis=1)
    attn_rows = gather_direct(attn_rows, "grp", grp_index).reshape(own_rows, -1)
    attn_rows = attn_rows.astype(jnp.float32)
    share_query = attn_rows[:, :width]
    share_out = attn_rows[:, width : 2 * width]
    share_pair = attn_rows[:, 2 * width : 2 * width + 2 * HD]
    share_gain_one = attn_rows[:, 2 * width + 2 * HD]
    share_gain_two = attn_rows[:, 2 * width + 2 * HD + 1]

    result = middle + scatter_ring(row_blocks(matmul(hidden, w_down)), "seq")
    layer_output = result.astype(jnp.bfloat16)[None, None]
    return (
        layer_output,
        input_grad[None, None],
        share_gain_one,
        share_query,
        share_pair,
        share_out,
        share_gain_two,
        share_gate,
        share_upper,
        share_down,
    )


def solution(mesh):
    by_row = P(("seq", "shard"), None)
    by_entry = P(("seq", "shard"))
    by_token = P("grp", "shard", "seq", None)
    return jax.shard_map(
        shards,
        mesh=mesh,
        in_specs=(
            by_token,
            P("grp", None),
            P("grp", None),
            by_entry,
            by_row,
            by_row,
            by_row,
            by_entry,
            by_row,
            by_row,
            by_row,
            by_token,
        ),
        out_specs=(
            by_token,
            by_token,
            by_entry,
            by_row,
            by_row,
            by_row,
            by_entry,
            by_row,
            by_row,
            by_row,
        ),
        check_vma=False,
    )
```

```python
import functools

import jax
import jax.numpy as jnp
from jax import lax
from jax.experimental import pallas as pl
from jax.experimental.pallas import tpu as pltpu
from jax.sharding import PartitionSpec as P

HEADS = 16
HD = 128
WINDOW = 1024
RING = 4
BLOCK = 128
CHUNK = 32
FBLOCK = 512

epsilon = 1e-06
big_negative = -1e30


def send(value, axis, steps):
    count = lax.axis_size(axis)
    return lax.ppermute(value, axis, [(i, (i + steps) % count) for i in range(count)])


def send_x(value, steps):
    return lax.ppermute(
        value,
        "shard",
        [(x * 2 + c, (x + steps) % RING * 2 + c) for x in range(RING) for c in range(2)],
    )


def send_core(value):
    return lax.ppermute(
        value, "shard", [(x * 2 + c, x * 2 + 1 - c) for x in range(RING) for c in range(2)]
    )


def fence(*values):
    return lax.optimization_barrier(values)


def shifted(value, axis, steps):
    count = lax.axis_size(axis)
    initial, last = (max(0, -steps), min(count, count - steps))
    return lax.ppermute(value, axis, [(i, i + steps) for i in range(initial, last)])


def gather_ring(piece, axis):
    half = piece.shape[0] // 2
    after = send(piece, axis, -1)
    before = send(piece, axis, 1)
    far_a = send(after[:half], axis, -1)
    far_b = send(before[half:], axis, 1)
    return [piece, after, jnp.concatenate([far_a, far_b], axis=0), before]


def scatter_ring(parts, axis):
    far = parts[2]
    own, nxt, prv = [parts[i].astype(jnp.float32) for i in (0, 1, 3)]
    half = own.shape[0] // 2
    got_a = send(far[:half].astype(jnp.bfloat16), axis, 1).astype(jnp.float32)
    got_b = send(far[half:].astype(jnp.bfloat16), axis, -1).astype(jnp.float32)
    nxt = jnp.concatenate([nxt[:half] + got_a, nxt[half:]], axis=0)
    prv = jnp.concatenate([prv[:half], prv[half:] + got_b], axis=0)
    from_prv = send(nxt.astype(jnp.bfloat16), axis, 1).astype(jnp.float32)
    from_nxt = send(prv.astype(jnp.bfloat16), axis, -1).astype(jnp.float32)
    return own + from_prv + from_nxt


def scatter_direct(pick, axis, index):
    got = [send(pick((index + k) % RING).astype(jnp.bfloat16), axis, k) for k in range(1, RING)]
    return pick(index) + sum(one.astype(jnp.float32) for one in got)


def gather_direct(piece, axis, index):
    got = [send(piece, axis, -k) for k in range(1, RING)]
    return ordered([piece] + got, index)


def scatter_x(pick, index):
    parts = [pick((index + k) % RING) for k in range(RING)]
    got = [send_x(parts[k].astype(jnp.bfloat16), k) for k in range(1, RING)]
    return parts[0] + sum(one.astype(jnp.float32) for one in got)


def ordered(parts, index):
    return jnp.stack(
        [
            lax.select_n(index, *[parts[(place - m) % RING] for m in range(RING)])
            for place in range(RING)
        ],
        axis=0,
    )


def exchange_parts(pick, axis, index):
    got = [pick((index + k) % RING) for k in range(RING)]
    return [got[0]] + [send(got[k], axis, k) for k in range(1, RING)]


def by_source(got, index):
    return ordered([got[0], got[3], got[2], got[1]], index)


def exchange(pick, axis, index):
    return by_source(exchange_parts(pick, axis, index), index)


def row_blocks(total):
    rows = total.shape[0] // RING
    return [total[i * rows : (i + 1) * rows] for i in range(RING)]


def norm_scale(values):
    return lax.rsqrt(jnp.mean(values * values, axis=-1, keepdims=True) + epsilon)


def norm_back(values, scale, gain, grad):
    scaled = grad * gain
    dot = jnp.mean(scaled * values, axis=-1, keepdims=True)
    return scaled * scale - values * (scale * scale * scale * dot)


def slot_starts(lengths, packing):
    slots = jnp.arange(lengths.shape[0], dtype=jnp.int32)
    picked = (packing[:, None] == slots[None, :]).astype(jnp.int32)
    packed = jnp.sum(picked * lengths[None, :], axis=1, dtype=jnp.int32)
    return jnp.cumsum(packed, dtype=jnp.int32) - packed


def rotation(place):
    half_width = HD // 2
    frequency = 10000.0 ** (-jnp.arange(half_width, dtype=jnp.float32) / half_width)
    angle = place.astype(jnp.float32)[:, None] * frequency
    cosine, sine = jnp.cos(angle), jnp.sin(angle)
    return jnp.concatenate([cosine, cosine], axis=1), jnp.concatenate([-sine, sine], axis=1)


def matmul(left, right):
    return jnp.dot(left, right, preferred_element_type=jnp.float32)


def inner_rows(left, right):
    return lax.dot_general(
        left, right, (((0,), (0,)), ((), ())), preferred_element_type=jnp.float32
    )


def inner_cols(left, right):
    return lax.dot_general(
        left, right, (((1,), (1,)), ((), ())), preferred_element_type=jnp.float32
    )


def tile_mask(info, tile, first_row, rows, reach, group):
    shard, seq = info[0], info[1]
    base = shard * group
    row = lax.broadcasted_iota(jnp.int32, (rows, 1), 0) + first_row
    query = base + (seq + tile) % RING * BLOCK + row
    begin = jnp.zeros_like(query)
    for slot in range(info.shape[0] - 2):
        start = info[2 + slot]
        begin = jnp.where(query >= start, jnp.maximum(begin, start), begin)
    lowest = jnp.maximum(begin, query - (WINDOW - 1))
    lane = lax.broadcasted_iota(jnp.int32, (1, reach), 1)
    block = lane // group
    in_block = lane - block * group
    key = base + (block - (reach // group - 1)) * group
    key = key + (seq + in_block // BLOCK) % RING * BLOCK + in_block % BLOCK
    return (key <= query) & (key >= lowest)


def attend_kernel(info, q_ref, *refs, heads, group):
    kv_refs, (out_ref, lse_ref, scores_ref, soft_ref) = refs[:-4], refs[-4:]
    reach = group * len(kv_refs)
    tile = pl.program_id(0)
    q = jnp.concatenate([q_ref[:, h * HD : (h + 1) * HD] for h in range(heads)], axis=0)
    for b, kv in enumerate(kv_refs):
        scores_ref[:, b * group : (b + 1) * group] = inner_cols(q, kv[:, :HD])
    for part in range(BLOCK // CHUNK):
        mask = tile_mask(info, tile, part * CHUNK, CHUNK, reach, group)
        for h in range(heads):
            at = pl.ds(h * BLOCK + part * CHUNK, CHUNK)
            scores = jnp.where(mask, scores_ref[at, :] * (HD**-0.5), big_negative)
            top = jnp.max(scores, axis=1, keepdims=True)
            expo = jnp.exp(scores - top)
            total = jnp.sum(expo, axis=1, keepdims=True)
            soft_ref[at, :] = (expo * (1.0 / total)).astype(jnp.bfloat16)
            lse_ref[0, at, :] = jnp.broadcast_to(top + jnp.log(total), (CHUNK, HD))
    acc = None
    for b, kv in enumerate(kv_refs):
        term = jnp.dot(soft_ref[:, b * group : (b + 1) * group], kv[:, HD:], preferred_element_type=jnp.float32)
        acc = term if acc is None else acc + term
    for h in range(heads):
        out_ref[:, h * HD : (h + 1) * HD] = acc[h * BLOCK : (h + 1) * BLOCK].astype(jnp.bfloat16)


def attend(info, queries, kvs):
    group, width = queries.shape
    heads = width // HD
    reach = group * len(kvs)
    whole = pl.BlockSpec((group, 2 * HD), lambda i: (0, 0))
    rows = pl.BlockSpec((BLOCK, width), lambda i: (i, 0))
    return pl.pallas_call(
        functools.partial(attend_kernel, heads=heads, group=group),
        grid=(group // BLOCK,),
        in_specs=[pl.BlockSpec(memory_space=pltpu.SMEM), rows] + [whole] * len(kvs),
        out_specs=[rows, pl.BlockSpec((1, heads * BLOCK, HD), lambda i: (i, 0, 0))],
        out_shape=[
            jax.ShapeDtypeStruct((group, width), jnp.bfloat16),
            jax.ShapeDtypeStruct((group // BLOCK, heads * BLOCK, HD), jnp.float32),
        ],
        scratch_shapes=[
            pltpu.VMEM((heads * BLOCK, reach), jnp.float32),
            pltpu.VMEM((heads * BLOCK, reach), jnp.bfloat16),
        ],
        compiler_params=pltpu.CompilerParams(vmem_limit_bytes=40 * 1024 * 1024),
        name="attend",
    )(info, queries, *kvs)


def attend_back_kernel(info, q_ref, do_ref, lse_ref, cos_ref, sin_ref, *refs, heads, group):
    count = len(refs) - 6
    kv_refs, (dq_ref, dkv_ref, scores_ref, dsoft_ref, soft_ref, dscores_ref) = refs[:count], refs[count:]
    reach = group * count
    tile = pl.program_id(0)

    @pl.when(tile == 0)
    def _():
        dkv_ref[...] = jnp.zeros_like(dkv_ref)

    q = jnp.concatenate([q_ref[:, h * HD : (h + 1) * HD] for h in range(heads)], axis=0)
    do = jnp.concatenate([do_ref[:, h * HD : (h + 1) * HD] for h in range(heads)], axis=0)
    for b, kv in enumerate(kv_refs):
        at = slice(b * group, (b + 1) * group)
        scores_ref[:, at] = inner_cols(q, kv[:, :HD])
        dsoft_ref[:, at] = inner_cols(do, kv[:, HD:])
    for part in range(BLOCK // CHUNK):
        mask = tile_mask(info, tile, part * CHUNK, CHUNK, reach, group)
        for h in range(heads):
            at = pl.ds(h * BLOCK + part * CHUNK, CHUNK)
            lse = lse_ref[0, at, 0:1]
            scores = jnp.where(mask, scores_ref[at, :] * (HD**-0.5), big_negative)
            soft = jnp.exp(scores - lse)
            dsoft = dsoft_ref[at, :]
            delta = jnp.sum(soft * dsoft, axis=1, keepdims=True)
            soft_ref[at, :] = soft.astype(jnp.bfloat16)
            dscores_ref[at, :] = (soft * (dsoft - delta)).astype(jnp.bfloat16)
    dq = None
    for b, kv in enumerate(kv_refs):
        at = slice(b * group, (b + 1) * group)
        term = jnp.dot(dscores_ref[:, at], kv[:, :HD], preferred_element_type=jnp.float32)
        dq = term if dq is None else dq + term
        dkv_ref[b, :, :HD] += inner_rows(dscores_ref[:, at], q) * (HD**-0.5)
        dkv_ref[b, :, HD:] += inner_rows(soft_ref[:, at], do)
    cos, sin = cos_ref[...], sin_ref[...]
    for h in range(heads):
        one = dq[h * BLOCK : (h + 1) * BLOCK] * (HD**-0.5)
        one = one * cos - pltpu.roll(one, HD // 2, 1) * sin
        dq_ref[:, h * HD : (h + 1) * HD] = one.astype(jnp.bfloat16)


def attend_back(info, queries, grads, lse, cos, sin, kvs):
    group, width = queries.shape
    heads = width // HD
    reach = group * len(kvs)
    whole = pl.BlockSpec((group, 2 * HD), lambda i: (0, 0))
    rows = pl.BlockSpec((BLOCK, width), lambda i: (i, 0))
    table = pl.BlockSpec((BLOCK, HD), lambda i: (i, 0))
    return pl.pallas_call(
        functools.partial(attend_back_kernel, heads=heads, group=group),
        grid=(group // BLOCK,),
        in_specs=[
            pl.BlockSpec(memory_space=pltpu.SMEM),
            rows,
            rows,
            pl.BlockSpec((1, heads * BLOCK, HD), lambda i: (i, 0, 0)),
            table,
            table,
        ]
        + [whole] * len(kvs),
        out_specs=[rows, pl.BlockSpec((len(kvs), group, 2 * HD), lambda i: (0, 0, 0))],
        out_shape=[
            jax.ShapeDtypeStruct((group, width), jnp.bfloat16),
            jax.ShapeDtypeStruct((len(kvs), group, 2 * HD), jnp.float32),
        ],
        scratch_shapes=[
            pltpu.VMEM((heads * BLOCK, reach), jnp.float32),
            pltpu.VMEM((heads * BLOCK, reach), jnp.float32),
            pltpu.VMEM((heads * BLOCK, reach), jnp.bfloat16),
            pltpu.VMEM((heads * BLOCK, reach), jnp.bfloat16),
        ],
        compiler_params=pltpu.CompilerParams(vmem_limit_bytes=40 * 1024 * 1024),
        name="attend_back",
    )(info, queries, grads, lse, cos, sin, *kvs)


def project_kernel(
    info, tok_ref, cos_ref, sin_ref, own, after, far_a, far_b, before, near, far,
    n_ref, q_ref, kv_ref, scale_ref, gains_ref, w_ref, sems, *, heads, block
):
    q_cols = heads * HD

    @pl.when(pl.program_id(0) == 0)
    def _():
        x, core, seq = info[0] // 2, info[0] % 2, info[1]
        copies = []

        def fetch(piece, k, other, first):
            place = (x + k) % RING * 2 + (1 - core if other else core)
            for i in range(piece.shape[0]):
                source = (seq - first - i + RING) % RING
                at = pl.multiple_of(source * 8 * block + place * block, block)
                copies.append(
                    pltpu.make_async_copy(
                        piece.at[i], w_ref.at[pl.ds(at, block), :], sems.at[len(copies)]
                    )
                )

        half = RING // 2
        fetch(own, 0, False, 0)
        fetch(after, 1, False, 0)
        fetch(far_a, 2, False, 0)
        fetch(far_b, 2, False, half)
        fetch(before, 3, False, 0)
        fetch(near.at[0], 0, True, 0)
        fetch(near.at[1], 1, True, 0)
        fetch(far, 2, True, 0)
        fetch(near.at[2], 3, True, 0)
        for copy in copies:
            copy.start()
        for copy in copies:
            copy.wait()
        pick = lax.broadcasted_iota(jnp.int32, (8, HD), 0) == lax.broadcasted_iota(
            jnp.int32, (8, HD), 1
        )
        gains_ref[...] = inner_cols(pick.astype(jnp.bfloat16), w_ref[:, q_cols + 2 * HD :])

    x = tok_ref[...].astype(jnp.float32)
    scale = lax.rsqrt(jnp.mean(x * x, axis=1, keepdims=True) + epsilon)
    normed = (x * scale * gains_ref[0:1, :]).astype(jnp.bfloat16)
    n_ref[...] = normed
    scale_ref[...] = jnp.broadcast_to(scale, scale_ref.shape)
    qkv = jnp.dot(normed, w_ref[:, : q_cols + 2 * HD], preferred_element_type=jnp.float32)
    cos, sin = cos_ref[...], sin_ref[...]
    for h in range(heads + 1):
        one = qkv[:, h * HD : (h + 1) * HD]
        one = (one * cos + pltpu.roll(one, HD // 2, 1) * sin).astype(jnp.bfloat16)
        if h < heads:
            q_ref[:, h * HD : (h + 1) * HD] = one
        else:
            kv_ref[:, :HD] = one
    kv_ref[:, HD:] = qkv[:, (heads + 1) * HD :].astype(jnp.bfloat16)


def project(info, tokens, cos, sin, pieces):
    group, width = tokens.shape
    block, columns = pieces[0].shape[1:]
    heads = columns // HD - 3
    rows = lambda n: pl.BlockSpec((BLOCK, n), lambda i: (i, 0))
    whole = lambda shape: pl.BlockSpec(shape, lambda i: (0, 0))
    return pl.pallas_call(
        functools.partial(project_kernel, heads=heads, block=block),
        grid=(group // BLOCK,),
        in_specs=[pl.BlockSpec(memory_space=pltpu.SMEM), rows(width), rows(HD), rows(HD)]
        + [pl.BlockSpec(memory_space=pl.ANY)] * len(pieces),
        out_specs=[
            rows(width),
            rows(heads * HD),
            rows(2 * HD),
            rows(HD),
            whole((8, width)),
            whole((width, columns)),
        ],
        out_shape=[
            jax.ShapeDtypeStruct((group, width), jnp.bfloat16),
            jax.ShapeDtypeStruct((group, heads * HD), jnp.bfloat16),
            jax.ShapeDtypeStruct((group, 2 * HD), jnp.bfloat16),
            jax.ShapeDtypeStruct((group, HD), jnp.float32),
            jax.ShapeDtypeStruct((8, width), jnp.float32),
            jax.ShapeDtypeStruct((width, columns), jnp.bfloat16),
        ],
        scratch_shapes=[pltpu.SemaphoreType.DMA((8 * RING,))],
        compiler_params=pltpu.CompilerParams(vmem_limit_bytes=40 * 1024 * 1024),
        name="project",
    )(info, tokens, cos, sin, *pieces)


def unproject_kernel(
    dq_ref, dkv_ref, w_ref, n_ref, tok_ref, scale_ref, att_ref, branch_ref, two_ref,
    part_ref, grad_ref
):
    q_cols = dq_ref.shape[1]
    n_attn = w_ref.shape[1]
    grads = jnp.concatenate([dq_ref[...], dkv_ref[...]], axis=1)
    part = inner_cols(grads, w_ref[:, : q_cols + 2 * HD])
    part_ref[...] = part.astype(jnp.bfloat16)
    terms = (part * tok_ref[...].astype(jnp.float32) * scale_ref[:, 0:1]).astype(jnp.bfloat16)
    column = lax.broadcasted_iota(jnp.int32, (part.shape[0], HD), 1)
    first = (column == 0).astype(jnp.bfloat16)
    second = (column == 1).astype(jnp.bfloat16)[: two_ref.shape[0]]
    grad_ref[:, : q_cols + 2 * HD] = inner_rows(n_ref[...], grads).astype(jnp.bfloat16)
    gains = inner_rows(terms, first) + inner_rows(two_ref[...], second)
    grad_ref[:, q_cols + 2 * HD : n_attn] = gains.astype(jnp.bfloat16)
    grad_ref[:, n_attn:] = inner_rows(att_ref[...], branch_ref[...]).astype(jnp.bfloat16)


def unproject(
    grad_queries, grad_pair, weights, normed, tokens, scale, attended, grad_branch, two
):
    group, width = tokens.shape
    size = 4 * BLOCK
    columns = weights.shape[1]
    whole = lambda n: pl.BlockSpec((group, n), lambda i: (0, 0))
    across = pl.BlockSpec((group, size), lambda i: (0, i))
    down = pl.BlockSpec((size, columns), lambda i: (i, 0))
    return pl.pallas_call(
        unproject_kernel,
        grid=(width // size,),
        in_specs=[
            whole(grad_queries.shape[1]),
            whole(grad_pair.shape[1]),
            down,
            across,
            across,
            whole(HD),
            whole(attended.shape[1]),
            across,
            pl.BlockSpec((two.shape[0], size), lambda i: (0, i)),
        ],
        out_specs=[across, pl.BlockSpec((size, columns + size), lambda i: (i, 0))],
        out_shape=[
            jax.ShapeDtypeStruct((group, width), jnp.bfloat16),
            jax.ShapeDtypeStruct((width, columns + size), jnp.bfloat16),
        ],
        compiler_params=pltpu.CompilerParams(vmem_limit_bytes=40 * 1024 * 1024),
        name="unproject",
    )(grad_queries, grad_pair, weights, normed, tokens, scale, attended, grad_branch, two)


def feed_kernel(n_ref, gh_ref, gate_ref, up_ref, hidden_ref, grad_ref):
    step = pl.program_id(0)
    size = gate_ref.shape[1]
    inner = grad_ref.shape[1] // 2
    gate = jnp.dot(n_ref[...], gate_ref[...], preferred_element_type=jnp.float32)
    upper = jnp.dot(n_ref[...], up_ref[...], preferred_element_type=jnp.float32)
    grad_hidden = gh_ref[...]
    root, cube = 0.7978845608028654, 0.044715
    square = gate * gate
    bend = jnp.tanh(root * gate * (1.0 + cube * square))
    half = 0.5 * (1.0 + bend)
    act = gate * half
    slope = half + 0.5 * gate * (1.0 - bend * bend) * (root * (1.0 + 3.0 * cube * square))
    hidden_ref[...] = (act * upper).astype(jnp.bfloat16)
    grad_gate = (grad_hidden * upper * slope).astype(jnp.bfloat16)
    grad_upper = (grad_hidden * act).astype(jnp.bfloat16)
    grad_ref[:, pl.ds(pl.multiple_of(step * size, size), size)] = grad_gate
    grad_ref[:, pl.ds(pl.multiple_of(inner + step * size, size), size)] = grad_upper


def feed(normed, grad_hidden, weights):
    group, width = normed.shape
    inner = grad_hidden.shape[1]
    steps = inner // FBLOCK
    whole = lambda n: pl.BlockSpec((group, n), lambda i: (0, 0))
    columns = pl.BlockSpec((group, FBLOCK), lambda i: (0, i))
    return pl.pallas_call(
        feed_kernel,
        grid=(steps,),
        in_specs=[
            whole(width),
            columns,
            pl.BlockSpec((width, FBLOCK), lambda i: (0, i)),
            pl.BlockSpec((width, FBLOCK), lambda i: (0, steps + i)),
        ],
        out_specs=[columns, whole(2 * inner)],
        out_shape=[
            jax.ShapeDtypeStruct((group, inner), jnp.bfloat16),
            jax.ShapeDtypeStruct((group, 2 * inner), jnp.bfloat16),
        ],
        compiler_params=pltpu.CompilerParams(vmem_limit_bytes=48 * 1024 * 1024),
        name="feed",
    )(normed, grad_hidden, weights, weights)


def back_kernel(left_ref, right_ref, out_ref):
    out_ref[...] = inner_cols(left_ref[...], right_ref[...]).astype(jnp.bfloat16)


def back(left, right):
    rows, inner = left.shape
    columns = right.shape[0]
    size = 2 * BLOCK
    return pl.pallas_call(
        back_kernel,
        grid=(columns // size,),
        in_specs=[
            pl.BlockSpec((rows, inner), lambda i: (0, 0)),
            pl.BlockSpec((size, inner), lambda i: (i, 0)),
        ],
        out_specs=pl.BlockSpec((rows, size), lambda i: (0, i)),
        out_shape=jax.ShapeDtypeStruct((rows, columns), jnp.bfloat16),
        compiler_params=pltpu.CompilerParams(vmem_limit_bytes=40 * 1024 * 1024),
        name="back",
    )(left, right)


def outer_kernel(left_ref, right_ref, out_ref):
    out_ref[...] = inner_rows(left_ref[...], right_ref[...]).astype(jnp.bfloat16)


def outer(left, right):
    rows, wide = left.shape
    columns = right.shape[1]
    size = 2 * BLOCK
    return pl.pallas_call(
        outer_kernel,
        grid=(wide // size,),
        in_specs=[
            pl.BlockSpec((rows, size), lambda i: (0, i)),
            pl.BlockSpec((rows, columns), lambda i: (0, 0)),
        ],
        out_specs=pl.BlockSpec((size, columns), lambda i: (i, 0)),
        out_shape=jax.ShapeDtypeStruct((wide, columns), jnp.bfloat16),
        compiler_params=pltpu.CompilerParams(vmem_limit_bytes=40 * 1024 * 1024),
        name="outer",
    )(left, right)


def times_kernel(left_ref, right_ref, out_ref):
    out_ref[...] = jnp.dot(
        left_ref[...], right_ref[...], preferred_element_type=jnp.float32
    ).astype(jnp.bfloat16)


def times(left, right):
    rows, inner = left.shape
    columns = right.shape[1]
    size = 4 * BLOCK
    return pl.pallas_call(
        times_kernel,
        grid=(columns // size,),
        in_specs=[
            pl.BlockSpec((rows, inner), lambda i: (0, 0)),
            pl.BlockSpec((inner, size), lambda i: (0, i)),
        ],
        out_specs=pl.BlockSpec((rows, size), lambda i: (0, i)),
        out_shape=jax.ShapeDtypeStruct((rows, columns), jnp.bfloat16),
        compiler_params=pltpu.CompilerParams(vmem_limit_bytes=40 * 1024 * 1024),
        name="times",
    )(left, right)


def shards(
    tokens,
    seq_lengths,
    seq_order,
    norm_gain,
    query_weight,
    key_value_weight,
    out_weight,
    mlp_gain,
    gate_weight,
    up_weight,
    down_weight,
    cotangent,
):
    rows = tokens.shape[2]
    width = tokens.shape[3]
    group_rows = rows * RING
    q_cols = HEADS // RING * HD
    f_cols = gate_weight.shape[1] // RING
    own_rows = query_weight.shape[0]
    shard_index = lax.axis_index("shard")
    seq_index = lax.axis_index("seq")
    grp_index = lax.axis_index("grp")
    own_tokens = tokens[0, 0]
    own_cotangent = cotangent[0, 0]

    gains = jnp.pad(jnp.stack([norm_gain, mlp_gain], axis=1), ((0, 0), (0, HD - 2)))

    def pick_q(i):
        own = lax.dynamic_slice_in_dim(query_weight, i * q_cols, q_cols, 1)
        return jnp.concatenate([own, key_value_weight, gains], axis=1)

    def pick_f(i):
        return jnp.concatenate(
            [
                lax.dynamic_slice_in_dim(gate_weight, i * f_cols, f_cols, 1),
                lax.dynamic_slice_in_dim(up_weight, i * f_cols, f_cols, 1),
            ],
            axis=1,
        )

    group_start = shard_index * group_rows
    ring_rows = (seq_index + jnp.arange(RING, dtype=jnp.int32)) % RING * rows
    in_group = (ring_rows[:, None] + jnp.arange(rows, dtype=jnp.int32)[None, :]).reshape(-1)
    query_index = group_start + in_group
    starts = slot_starts(seq_lengths[0], seq_order[0])
    begins = jnp.max(
        jnp.where(query_index[:, None] >= starts[None, :], starts[None, :], 0), axis=1
    )
    cos, sin = rotation(query_index - begins)
    info = jnp.concatenate([jnp.stack([shard_index, seq_index]).astype(jnp.int32), starts])

    def scattered(grad, dim):
        return lax.psum_scatter(grad, "shard", scatter_dimension=dim, tiled=True)

    w_out = lax.all_gather(out_weight, "shard", axis=0, tiled=True)
    got = exchange_parts(pick_q, "seq", seq_index)
    tok_after = send(own_tokens, "seq", -1)
    tok_before = send(own_tokens, "seq", 1)
    *got, tok_after, tok_before, gate_weight, up_weight, down_weight = fence(
        *got, tok_after, tok_before, gate_weight, up_weight, down_weight
    )
    w_down = lax.all_gather(down_weight, "shard", axis=0, tiled=True)
    block = jnp.stack(got)
    block_after = send_x(block, -1)
    block_before = send_x(block, 1)
    half = rows // 2
    tok_far_a = send(tok_after[:half], "seq", -1)
    tok_far_b = send(tok_before[half:], "seq", 1)
    block_after, block_before, tok_far_a, tok_far_b, gate_weight, up_weight, w_out = fence(
        block_after, block_before, tok_far_a, tok_far_b, gate_weight, up_weight, w_out
    )
    block_far_a = send_x(block_after[: RING // 2], -1)
    block_far_b = send_x(block_before[RING // 2 :], 1)
    near = send_core(jnp.stack([block, block_after, block_before]))
    got = exchange_parts(pick_f, "seq", seq_index)
    tokens_bf = jnp.concatenate([own_tokens, tok_after, tok_far_a, tok_far_b, tok_before], axis=0)
    block_far_a, block_far_b, near, tokens_bf = fence(block_far_a, block_far_b, near, tokens_bf)
    far = send_core(jnp.concatenate([block_far_a, block_far_b]))
    pieces = (block, block_after, block_far_a, block_far_b, block_before, near, far)
    normed_one, queries, pair, scale_one, gain_rows, w_attn = project(
        info, tokens_bf, cos, sin, pieces
    )
    *got, own_cotangent, pair = fence(*got, own_cotangent, pair)
    w_ff = lax.all_gather(by_source(got, seq_index), "shard", axis=1, tiled=True)
    w_ff = w_ff.reshape(width, -1)
    kvs = [shifted(pair, "shard", 2), shifted(pair, "shard", 1), pair]
    *kvs, own_cotangent = fence(*kvs, own_cotangent)
    cot_after = send(own_cotangent, "seq", -1)
    cot_before = send(own_cotangent, "seq", 1)
    gain_one, gain_two = gain_rows[0], gain_rows[1]
    attended, lse = attend(info, queries, kvs)
    attended, cot_after, cot_before, w_down = fence(attended, cot_after, cot_before, w_down)
    cot_far_a = send(cot_after[:half], "seq", -1)
    cot_far_b = send(cot_before[half:], "seq", 1)
    all_cotangent = jnp.concatenate(
        [own_cotangent, cot_after, cot_far_a, cot_far_b, cot_before], axis=0
    )

    branch = scatter_ring(row_blocks(matmul(attended, w_out)), "seq")
    middle = own_tokens.astype(jnp.float32) + branch
    scale_two = norm_scale(middle)
    normed_two = (middle * scale_two * gain_two).astype(jnp.bfloat16)
    normed_two = jnp.concatenate(gather_ring(normed_two, "seq"), axis=0)
    grad_hidden, normed_two = fence(inner_cols(all_cotangent, w_down), normed_two)
    hidden, grad_ff = feed(normed_two, grad_hidden, w_ff)
    grad_down = outer(hidden, all_cotangent)
    share_down = scattered(grad_down, 0)
    grad_down, grad_ff = fence(grad_down, grad_ff)
    partial_two = back(grad_ff, w_ff)
    part = own_rows // RING

    def first_half(parts):
        return send(parts[2][:half], "seq", 1), send(parts[2][half:], "seq", -1)

    def second_half(parts, got_a, got_b):
        one, last = [parts[i].astype(jnp.float32) for i in (1, 3)]
        one = jnp.concatenate([one[:half] + got_a.astype(jnp.float32), one[half:]], axis=0)
        last = jnp.concatenate([last[:half], last[half:] + got_b.astype(jnp.float32)], axis=0)
        return (
            send(one.astype(jnp.bfloat16), "seq", 1),
            send(last.astype(jnp.bfloat16), "seq", -1),
        )

    def total(*blocks):
        return sum(block.astype(jnp.float32) for block in blocks)

    parts = row_blocks(partial_two)
    two_a, two_b = first_half(parts)
    two_a, two_b, grad_ff = fence(two_a, two_b, grad_ff)
    from_last, from_next = second_half(parts, two_a, two_b)
    grad_wff = outer(normed_two, grad_ff)
    from_last, from_next, grad_wff, hidden = fence(from_last, from_next, grad_wff, hidden)
    share_ff = scattered(grad_wff.reshape(RING, -1, 2 * f_cols), 1)
    grad_normed_two = total(parts[0], from_last, from_next)
    grad_middle = own_cotangent.astype(jnp.float32) + norm_back(
        middle, scale_two, gain_two, grad_normed_two
    )
    own_branch = grad_middle.astype(jnp.bfloat16)

    gb_after = send(own_branch, "seq", -1)
    gb_before = send(own_branch, "seq", 1)
    out_parts = times(hidden, w_down)
    gb_after, gb_before, out_parts = fence(gb_after, gb_before, out_parts)
    out_parts = row_blocks(out_parts)
    gb_far_a = send(gb_after[:half], "seq", -1)
    gb_far_b = send(gb_before[half:], "seq", 1)
    gb_far_a, gb_far_b, *out_parts = fence(gb_far_a, gb_far_b, *out_parts)
    grad_branch = jnp.concatenate([own_branch, gb_after, gb_far_a, gb_far_b, gb_before], axis=0)
    grad_attended = inner_cols(grad_branch, w_out).astype(jnp.bfloat16)

    out_a, out_b = first_half(out_parts)
    grad_queries, grad_table = attend_back(info, queries, grad_attended, lse, cos, sin, kvs)
    grad_queries, grad_table, out_a, out_b, share_down = fence(
        grad_queries, grad_table, out_a, out_b, share_down
    )

    returned_two = shifted(grad_table[0].astype(jnp.bfloat16), "shard", -2)
    returned_one = shifted(grad_table[1].astype(jnp.bfloat16), "shard", -1)

    def grp_pieces(share, dim):
        return exchange_parts(
            lambda i: lax.dynamic_index_in_dim(share, i, dim, keepdims=False), "grp", grp_index
        )

    def seq_pieces(summed):
        return exchange_parts(
            lambda i: lax.dynamic_index_in_dim(summed, i, 0, keepdims=False), "seq", seq_index
        )

    def side_by_side(columns):
        return columns.transpose(1, 0, 2).reshape(columns.shape[1], -1)

    down_pieces = grp_pieces(share_down.reshape(RING, -1, width), 0)
    returned_one, returned_two, grad_table, out_a, out_b, *down_pieces = fence(
        returned_one, returned_two, grad_table, out_a, out_b, *down_pieces
    )
    grad_pair = total(grad_table[2], returned_one, returned_two)
    grad_keys = grad_pair[:, :HD]
    swapped = jnp.concatenate([grad_keys[:, HD // 2 :], grad_keys[:, : HD // 2]], axis=1)
    grad_keys = grad_keys * cos - swapped * sin
    grad_pair = jnp.concatenate([grad_keys, grad_pair[:, HD:]], axis=1).astype(jnp.bfloat16)
    gain_two_terms = (grad_normed_two * middle * scale_two).astype(jnp.bfloat16)
    partial_one, grad_attn = unproject(
        grad_queries, grad_pair, w_attn, normed_one, tokens_bf, scale_one, attended, grad_branch,
        gain_two_terms,
    )
    parts = row_blocks(partial_one)
    one_a, one_b = first_half(parts)
    n_attn = w_attn.shape[1]
    share_attn = scattered(grad_attn.reshape(RING, -1, grad_attn.shape[1]), 1)
    down_own = total(*down_pieces).astype(jnp.bfloat16)
    down_got = [send(down_own, "grp", -k) for k in range(1, RING)]
    one_a, one_b, out_a, out_b, share_ff, *down_got = fence(
        one_a, one_b, out_a, out_b, share_ff, *down_got
    )
    from_last, from_next = second_half(parts, one_a, one_b)
    ff_pieces = grp_pieces(share_ff.reshape(RING, RING, part, -1), 1)
    from_last, from_next, out_a, out_b, *ff_pieces = fence(
        from_last, from_next, out_a, out_b, *ff_pieces
    )
    ff_pieces = seq_pieces(total(*ff_pieces).astype(jnp.bfloat16))
    out_last, out_next = second_half(out_parts, out_a, out_b)
    out_last, out_next, *ff_pieces = fence(out_last, out_next, *ff_pieces)
    result = middle + total(out_parts[0], out_last, out_next)
    layer_output = result.astype(jnp.bfloat16)[None, None]
    share_down = ordered([down_own] + down_got, grp_index).reshape(-1, width)
    share_down = share_down.astype(jnp.float32)
    ff_columns = by_source(ff_pieces, seq_index)
    ff_rows = jnp.concatenate(
        [side_by_side(ff_columns[:, :, :f_cols]), side_by_side(ff_columns[:, :, f_cols:])], axis=1
    )
    ff_after = send(ff_rows, "grp", -1)
    ff_before = send(ff_rows, "grp", 1)
    grad_normed_one = total(parts[0], from_last, from_next)
    own_inputs = own_tokens.astype(jnp.float32)
    input_grad = grad_middle + norm_back(
        own_inputs, norm_scale(own_inputs), gain_one, grad_normed_one
    )
    ff_after, ff_before, input_grad = fence(ff_after, ff_before, input_grad)
    ff_far_a = send(ff_after[: part // 2], "grp", -1)
    ff_far_b = send(ff_before[part // 2 :], "grp", 1)
    ff_far_a, ff_far_b, share_attn = fence(ff_far_a, ff_far_b, share_attn)
    pieces = grp_pieces(share_attn.reshape(RING, RING, part, -1), 1)
    ff_far = jnp.concatenate([ff_far_a, ff_far_b], axis=0)
    ff_rows = ordered([ff_rows, ff_after, ff_far, ff_before], grp_index)
    ff_rows = ff_rows.reshape(own_rows, -1).astype(jnp.float32)
    share_gate = ff_rows[:, : RING * f_cols]
    share_upper = ff_rows[:, RING * f_cols :]
    summed = total(*pieces).astype(jnp.bfloat16)
    out_own = side_by_side(summed[:, :, n_attn:])
    columns = by_source(seq_pieces(summed[:, :, :n_attn]), seq_index)
    summed = total(*[columns[i, :, q_cols:] for i in range(RING)]).astype(jnp.bfloat16)
    attn_rows = jnp.concatenate(
        [side_by_side(columns[:, :, :q_cols]), out_own, summed], axis=1
    )
    attn_rows = gather_direct(attn_rows, "grp", grp_index).reshape(own_rows, -1)
    attn_rows = attn_rows.astype(jnp.float32)
    share_query = attn_rows[:, :width]
    share_out = attn_rows[:, width : 2 * width]
    share_pair = attn_rows[:, 2 * width : 2 * width + 2 * HD]
    share_gain_one = attn_rows[:, 2 * width + 2 * HD]
    share_gain_two = attn_rows[:, 2 * width + 2 * HD + 1]
    return (
        layer_output,
        input_grad[None, None],
        share_gain_one,
        share_query,
        share_pair,
        share_out,
        share_gain_two,
        share_gate,
        share_upper,
        share_down,
    )


def solution(mesh):
    by_row = P(("seq", "shard"), None)
    by_entry = P(("seq", "shard"))
    by_token = P("grp", "shard", "seq", None)
    return jax.shard_map(
        shards,
        mesh=mesh,
        in_specs=(
            by_token,
            P("grp", None),
            P("grp", None),
            by_entry,
            by_row,
            by_row,
            by_row,
            by_entry,
            by_row,
            by_row,
            by_row,
            by_token,
        ),
        out_specs=(
            by_token,
            by_token,
            by_entry,
            by_row,
            by_row,
            by_row,
            by_entry,
            by_row,
            by_row,
            by_row,
        ),
        check_vma=False,
    )
```

```python
import functools

import jax
import jax.numpy as jnp
from jax import lax
from jax.experimental import pallas as pl
from jax.experimental.pallas import tpu as pltpu
from jax.sharding import PartitionSpec as P

HEADS = 16
HD = 128
WINDOW = 1024
RING = 4
BLOCK = 128
CHUNK = 32
FBLOCK = 512

epsilon = 1e-06
big_negative = -1e30


def send(value, axis, steps):
    count = lax.axis_size(axis)
    return lax.ppermute(value, axis, [(i, (i + steps) % count) for i in range(count)])


def send_x(value, steps):
    return lax.ppermute(
        value,
        "shard",
        [(x * 2 + c, (x + steps) % RING * 2 + c) for x in range(RING) for c in range(2)],
    )


def send_core(value):
    return lax.ppermute(
        value, "shard", [(x * 2 + c, x * 2 + 1 - c) for x in range(RING) for c in range(2)]
    )


def fence(*values):
    return lax.optimization_barrier(values)


def shifted(value, axis, steps):
    count = lax.axis_size(axis)
    initial, last = (max(0, -steps), min(count, count - steps))
    return lax.ppermute(value, axis, [(i, i + steps) for i in range(initial, last)])


def gather_ring(piece, axis):
    half = piece.shape[0] // 2
    after = send(piece, axis, -1)
    before = send(piece, axis, 1)
    far_a = send(after[:half], axis, -1)
    far_b = send(before[half:], axis, 1)
    return [piece, after, jnp.concatenate([far_a, far_b], axis=0), before]


def scatter_ring(parts, axis):
    far = parts[2]
    own, nxt, prv = [parts[i].astype(jnp.float32) for i in (0, 1, 3)]
    half = own.shape[0] // 2
    got_a = send(far[:half].astype(jnp.bfloat16), axis, 1).astype(jnp.float32)
    got_b = send(far[half:].astype(jnp.bfloat16), axis, -1).astype(jnp.float32)
    nxt = jnp.concatenate([nxt[:half] + got_a, nxt[half:]], axis=0)
    prv = jnp.concatenate([prv[:half], prv[half:] + got_b], axis=0)
    from_prv = send(nxt.astype(jnp.bfloat16), axis, 1).astype(jnp.float32)
    from_nxt = send(prv.astype(jnp.bfloat16), axis, -1).astype(jnp.float32)
    return own + from_prv + from_nxt


def scatter_direct(pick, axis, index):
    got = [send(pick((index + k) % RING).astype(jnp.bfloat16), axis, k) for k in range(1, RING)]
    return pick(index) + sum(one.astype(jnp.float32) for one in got)


def gather_direct(piece, axis, index):
    got = [send(piece, axis, -k) for k in range(1, RING)]
    return ordered([piece] + got, index)


def scatter_x(pick, index):
    parts = [pick((index + k) % RING) for k in range(RING)]
    got = [send_x(parts[k].astype(jnp.bfloat16), k) for k in range(1, RING)]
    return parts[0] + sum(one.astype(jnp.float32) for one in got)


def ordered(parts, index):
    return jnp.stack(
        [
            lax.select_n(index, *[parts[(place - m) % RING] for m in range(RING)])
            for place in range(RING)
        ],
        axis=0,
    )


def exchange_parts(pick, axis, index):
    got = [pick((index + k) % RING) for k in range(RING)]
    return [got[0]] + [send(got[k], axis, k) for k in range(1, RING)]


def by_source(got, index):
    return ordered([got[0], got[3], got[2], got[1]], index)


def exchange(pick, axis, index):
    return by_source(exchange_parts(pick, axis, index), index)


def row_blocks(total):
    rows = total.shape[0] // RING
    return [total[i * rows : (i + 1) * rows] for i in range(RING)]


def norm_scale(values):
    return lax.rsqrt(jnp.mean(values * values, axis=-1, keepdims=True) + epsilon)


def norm_back(values, scale, gain, grad):
    scaled = grad * gain
    dot = jnp.mean(scaled * values, axis=-1, keepdims=True)
    return scaled * scale - values * (scale * scale * scale * dot)


def slot_starts(lengths, packing):
    slots = jnp.arange(lengths.shape[0], dtype=jnp.int32)
    picked = (packing[:, None] == slots[None, :]).astype(jnp.int32)
    packed = jnp.sum(picked * lengths[None, :], axis=1, dtype=jnp.int32)
    return jnp.cumsum(packed, dtype=jnp.int32) - packed


def rotation(place):
    half_width = HD // 2
    frequency = 10000.0 ** (-jnp.arange(half_width, dtype=jnp.float32) / half_width)
    angle = place.astype(jnp.float32)[:, None] * frequency
    cosine, sine = jnp.cos(angle), jnp.sin(angle)
    return jnp.concatenate([cosine, cosine], axis=1), jnp.concatenate([-sine, sine], axis=1)


def matmul(left, right):
    return jnp.dot(left, right, preferred_element_type=jnp.float32)


def inner_rows(left, right):
    return lax.dot_general(
        left, right, (((0,), (0,)), ((), ())), preferred_element_type=jnp.float32
    )


def inner_cols(left, right):
    return lax.dot_general(
        left, right, (((1,), (1,)), ((), ())), preferred_element_type=jnp.float32
    )


def tile_mask(info, tile, first_row, rows, reach, group):
    shard, seq = info[0], info[1]
    base = shard * group
    row = lax.broadcasted_iota(jnp.int32, (rows, 1), 0) + first_row
    query = base + (seq + tile) % RING * BLOCK + row
    begin = jnp.zeros_like(query)
    for slot in range(info.shape[0] - 2):
        start = info[2 + slot]
        begin = jnp.where(query >= start, jnp.maximum(begin, start), begin)
    lowest = jnp.maximum(begin, query - (WINDOW - 1))
    lane = lax.broadcasted_iota(jnp.int32, (1, reach), 1)
    block = lane // group
    in_block = lane - block * group
    key = base + (block - (reach // group - 1)) * group
    key = key + (seq + in_block // BLOCK) % RING * BLOCK + in_block % BLOCK
    return (key <= query) & (key >= lowest)


def attend_kernel(info, q_ref, *refs, heads, group):
    kv_refs, (out_ref, lse_ref, scores_ref, soft_ref) = refs[:-4], refs[-4:]
    reach = group * len(kv_refs)
    tile = pl.program_id(0)
    q = jnp.concatenate([q_ref[:, h * HD : (h + 1) * HD] for h in range(heads)], axis=0)
    for b, kv in enumerate(kv_refs):
        scores_ref[:, b * group : (b + 1) * group] = inner_cols(q, kv[:, :HD])
    for part in range(BLOCK // CHUNK):
        mask = tile_mask(info, tile, part * CHUNK, CHUNK, reach, group)
        for h in range(heads):
            at = pl.ds(h * BLOCK + part * CHUNK, CHUNK)
            scores = jnp.where(mask, scores_ref[at, :] * (HD**-0.5), big_negative)
            top = jnp.max(scores, axis=1, keepdims=True)
            expo = jnp.exp(scores - top)
            total = jnp.sum(expo, axis=1, keepdims=True)
            soft_ref[at, :] = (expo * (1.0 / total)).astype(jnp.bfloat16)
            lse_ref[0, at, :] = jnp.broadcast_to(top + jnp.log(total), (CHUNK, HD))
    acc = None
    for b, kv in enumerate(kv_refs):
        term = jnp.dot(soft_ref[:, b * group : (b + 1) * group], kv[:, HD:], preferred_element_type=jnp.float32)
        acc = term if acc is None else acc + term
    for h in range(heads):
        out_ref[:, h * HD : (h + 1) * HD] = acc[h * BLOCK : (h + 1) * BLOCK].astype(jnp.bfloat16)


def attend(info, queries, kvs):
    group, width = queries.shape
    heads = width // HD
    reach = group * len(kvs)
    whole = pl.BlockSpec((group, 2 * HD), lambda i: (0, 0))
    rows = pl.BlockSpec((BLOCK, width), lambda i: (i, 0))
    return pl.pallas_call(
        functools.partial(attend_kernel, heads=heads, group=group),
        grid=(group // BLOCK,),
        in_specs=[pl.BlockSpec(memory_space=pltpu.SMEM), rows] + [whole] * len(kvs),
        out_specs=[rows, pl.BlockSpec((1, heads * BLOCK, HD), lambda i: (i, 0, 0))],
        out_shape=[
            jax.ShapeDtypeStruct((group, width), jnp.bfloat16),
            jax.ShapeDtypeStruct((group // BLOCK, heads * BLOCK, HD), jnp.float32),
        ],
        scratch_shapes=[
            pltpu.VMEM((heads * BLOCK, reach), jnp.float32),
            pltpu.VMEM((heads * BLOCK, reach), jnp.bfloat16),
        ],
        compiler_params=pltpu.CompilerParams(vmem_limit_bytes=40 * 1024 * 1024),
        name="attend",
    )(info, queries, *kvs)


def attend_back_kernel(info, q_ref, do_ref, lse_ref, cos_ref, sin_ref, *refs, heads, group):
    count = len(refs) - 6
    kv_refs, (dq_ref, dkv_ref, scores_ref, dsoft_ref, soft_ref, dscores_ref) = refs[:count], refs[count:]
    reach = group * count
    tile = pl.program_id(0)

    @pl.when(tile == 0)
    def _():
        dkv_ref[...] = jnp.zeros_like(dkv_ref)

    q = jnp.concatenate([q_ref[:, h * HD : (h + 1) * HD] for h in range(heads)], axis=0)
    do = jnp.concatenate([do_ref[:, h * HD : (h + 1) * HD] for h in range(heads)], axis=0)
    for b, kv in enumerate(kv_refs):
        at = slice(b * group, (b + 1) * group)
        scores_ref[:, at] = inner_cols(q, kv[:, :HD])
        dsoft_ref[:, at] = inner_cols(do, kv[:, HD:])
    for part in range(BLOCK // CHUNK):
        mask = tile_mask(info, tile, part * CHUNK, CHUNK, reach, group)
        for h in range(heads):
            at = pl.ds(h * BLOCK + part * CHUNK, CHUNK)
            lse = lse_ref[0, at, 0:1]
            scores = jnp.where(mask, scores_ref[at, :] * (HD**-0.5), big_negative)
            soft = jnp.exp(scores - lse)
            dsoft = dsoft_ref[at, :]
            delta = jnp.sum(soft * dsoft, axis=1, keepdims=True)
            soft_ref[at, :] = soft.astype(jnp.bfloat16)
            dscores_ref[at, :] = (soft * (dsoft - delta)).astype(jnp.bfloat16)
    dq = None
    for b, kv in enumerate(kv_refs):
        at = slice(b * group, (b + 1) * group)
        term = jnp.dot(dscores_ref[:, at], kv[:, :HD], preferred_element_type=jnp.float32)
        dq = term if dq is None else dq + term
        dkv_ref[b, :, :HD] += inner_rows(dscores_ref[:, at], q) * (HD**-0.5)
        dkv_ref[b, :, HD:] += inner_rows(soft_ref[:, at], do)
    cos, sin = cos_ref[...], sin_ref[...]
    for h in range(heads):
        one = dq[h * BLOCK : (h + 1) * BLOCK] * (HD**-0.5)
        one = one * cos - pltpu.roll(one, HD // 2, 1) * sin
        dq_ref[:, h * HD : (h + 1) * HD] = one.astype(jnp.bfloat16)


def attend_back(info, queries, grads, lse, cos, sin, kvs):
    group, width = queries.shape
    heads = width // HD
    reach = group * len(kvs)
    whole = pl.BlockSpec((group, 2 * HD), lambda i: (0, 0))
    rows = pl.BlockSpec((BLOCK, width), lambda i: (i, 0))
    table = pl.BlockSpec((BLOCK, HD), lambda i: (i, 0))
    return pl.pallas_call(
        functools.partial(attend_back_kernel, heads=heads, group=group),
        grid=(group // BLOCK,),
        in_specs=[
            pl.BlockSpec(memory_space=pltpu.SMEM),
            rows,
            rows,
            pl.BlockSpec((1, heads * BLOCK, HD), lambda i: (i, 0, 0)),
            table,
            table,
        ]
        + [whole] * len(kvs),
        out_specs=[rows, pl.BlockSpec((len(kvs), group, 2 * HD), lambda i: (0, 0, 0))],
        out_shape=[
            jax.ShapeDtypeStruct((group, width), jnp.bfloat16),
            jax.ShapeDtypeStruct((len(kvs), group, 2 * HD), jnp.float32),
        ],
        scratch_shapes=[
            pltpu.VMEM((heads * BLOCK, reach), jnp.float32),
            pltpu.VMEM((heads * BLOCK, reach), jnp.float32),
            pltpu.VMEM((heads * BLOCK, reach), jnp.bfloat16),
            pltpu.VMEM((heads * BLOCK, reach), jnp.bfloat16),
        ],
        compiler_params=pltpu.CompilerParams(vmem_limit_bytes=40 * 1024 * 1024),
        name="attend_back",
    )(info, queries, grads, lse, cos, sin, *kvs)


def project_kernel(
    info, tok_ref, cos_ref, sin_ref, own, after, far_a, far_b, before, near, far,
    n_ref, q_ref, kv_ref, scale_ref, gains_ref, w_ref, sems, *, heads, block
):
    q_cols = heads * HD

    @pl.when(pl.program_id(0) == 0)
    def _():
        x, core, seq = info[0] // 2, info[0] % 2, info[1]
        copies = []

        def fetch(piece, k, other, first):
            place = (x + k) % RING * 2 + (1 - core if other else core)
            for i in range(piece.shape[0]):
                source = (seq - first - i + RING) % RING
                at = pl.multiple_of(source * 8 * block + place * block, block)
                copies.append(
                    pltpu.make_async_copy(
                        piece.at[i], w_ref.at[pl.ds(at, block), :], sems.at[len(copies)]
                    )
                )

        half = RING // 2
        fetch(own, 0, False, 0)
        fetch(after, 1, False, 0)
        fetch(far_a, 2, False, 0)
        fetch(far_b, 2, False, half)
        fetch(before, 3, False, 0)
        fetch(near.at[0], 0, True, 0)
        fetch(near.at[1], 1, True, 0)
        fetch(far, 2, True, 0)
        fetch(near.at[2], 3, True, 0)
        for copy in copies:
            copy.start()
        for copy in copies:
            copy.wait()
        pick = lax.broadcasted_iota(jnp.int32, (8, HD), 0) == lax.broadcasted_iota(
            jnp.int32, (8, HD), 1
        )
        gains_ref[...] = inner_cols(pick.astype(jnp.bfloat16), w_ref[:, q_cols + 2 * HD :])

    x = tok_ref[...].astype(jnp.float32)
    scale = lax.rsqrt(jnp.mean(x * x, axis=1, keepdims=True) + epsilon)
    normed = (x * scale * gains_ref[0:1, :]).astype(jnp.bfloat16)
    n_ref[...] = normed
    scale_ref[...] = jnp.broadcast_to(scale, scale_ref.shape)
    qkv = jnp.dot(normed, w_ref[:, : q_cols + 2 * HD], preferred_element_type=jnp.float32)
    cos, sin = cos_ref[...], sin_ref[...]
    for h in range(heads + 1):
        one = qkv[:, h * HD : (h + 1) * HD]
        one = (one * cos + pltpu.roll(one, HD // 2, 1) * sin).astype(jnp.bfloat16)
        if h < heads:
            q_ref[:, h * HD : (h + 1) * HD] = one
        else:
            kv_ref[:, :HD] = one
    kv_ref[:, HD:] = qkv[:, (heads + 1) * HD :].astype(jnp.bfloat16)


def project(info, tokens, cos, sin, pieces):
    group, width = tokens.shape
    block, columns = pieces[0].shape[1:]
    heads = columns // HD - 3
    rows = lambda n: pl.BlockSpec((BLOCK, n), lambda i: (i, 0))
    whole = lambda shape: pl.BlockSpec(shape, lambda i: (0, 0))
    return pl.pallas_call(
        functools.partial(project_kernel, heads=heads, block=block),
        grid=(group // BLOCK,),
        in_specs=[pl.BlockSpec(memory_space=pltpu.SMEM), rows(width), rows(HD), rows(HD)]
        + [pl.BlockSpec(memory_space=pl.ANY)] * len(pieces),
        out_specs=[
            rows(width),
            rows(heads * HD),
            rows(2 * HD),
            rows(HD),
            whole((8, width)),
            whole((width, columns)),
        ],
        out_shape=[
            jax.ShapeDtypeStruct((group, width), jnp.bfloat16),
            jax.ShapeDtypeStruct((group, heads * HD), jnp.bfloat16),
            jax.ShapeDtypeStruct((group, 2 * HD), jnp.bfloat16),
            jax.ShapeDtypeStruct((group, HD), jnp.float32),
            jax.ShapeDtypeStruct((8, width), jnp.float32),
            jax.ShapeDtypeStruct((width, columns), jnp.bfloat16),
        ],
        scratch_shapes=[pltpu.SemaphoreType.DMA((8 * RING,))],
        compiler_params=pltpu.CompilerParams(vmem_limit_bytes=40 * 1024 * 1024),
        name="project",
    )(info, tokens, cos, sin, *pieces)


def unproject_kernel(
    dq_ref, dkv_ref, w_ref, n_ref, tok_ref, scale_ref, att_ref, branch_ref, two_ref,
    part_ref, grad_ref
):
    q_cols = dq_ref.shape[1]
    n_attn = w_ref.shape[1]
    grads = jnp.concatenate([dq_ref[...], dkv_ref[...]], axis=1)
    part = inner_cols(grads, w_ref[:, : q_cols + 2 * HD])
    part_ref[...] = part.astype(jnp.bfloat16)
    terms = (part * tok_ref[...].astype(jnp.float32) * scale_ref[:, 0:1]).astype(jnp.bfloat16)
    column = lax.broadcasted_iota(jnp.int32, (part.shape[0], HD), 1)
    first = (column == 0).astype(jnp.bfloat16)
    second = (column == 1).astype(jnp.bfloat16)[: two_ref.shape[0]]
    grad_ref[:, : q_cols + 2 * HD] = inner_rows(n_ref[...], grads).astype(jnp.bfloat16)
    gains = inner_rows(terms, first) + inner_rows(two_ref[...], second)
    grad_ref[:, q_cols + 2 * HD : n_attn] = gains.astype(jnp.bfloat16)
    grad_ref[:, n_attn:] = inner_rows(att_ref[...], branch_ref[...]).astype(jnp.bfloat16)


def unproject(
    grad_queries, grad_pair, weights, normed, tokens, scale, attended, grad_branch, two
):
    group, width = tokens.shape
    size = 4 * BLOCK
    columns = weights.shape[1]
    whole = lambda n: pl.BlockSpec((group, n), lambda i: (0, 0))
    across = pl.BlockSpec((group, size), lambda i: (0, i))
    down = pl.BlockSpec((size, columns), lambda i: (i, 0))
    return pl.pallas_call(
        unproject_kernel,
        grid=(width // size,),
        in_specs=[
            whole(grad_queries.shape[1]),
            whole(grad_pair.shape[1]),
            down,
            across,
            across,
            whole(HD),
            whole(attended.shape[1]),
            across,
            pl.BlockSpec((two.shape[0], size), lambda i: (0, i)),
        ],
        out_specs=[across, pl.BlockSpec((size, columns + size), lambda i: (i, 0))],
        out_shape=[
            jax.ShapeDtypeStruct((group, width), jnp.bfloat16),
            jax.ShapeDtypeStruct((width, columns + size), jnp.bfloat16),
        ],
        compiler_params=pltpu.CompilerParams(vmem_limit_bytes=40 * 1024 * 1024),
        name="unproject",
    )(grad_queries, grad_pair, weights, normed, tokens, scale, attended, grad_branch, two)


def feed_kernel(n_ref, gh_ref, gate_ref, up_ref, hidden_ref, grad_ref):
    step = pl.program_id(0)
    size = gate_ref.shape[1]
    inner = grad_ref.shape[1] // 2
    gate = jnp.dot(n_ref[...], gate_ref[...], preferred_element_type=jnp.float32)
    upper = jnp.dot(n_ref[...], up_ref[...], preferred_element_type=jnp.float32)
    grad_hidden = gh_ref[...]
    root, cube = 0.7978845608028654, 0.044715
    square = gate * gate
    bend = jnp.tanh(root * gate * (1.0 + cube * square))
    half = 0.5 * (1.0 + bend)
    act = gate * half
    slope = half + 0.5 * gate * (1.0 - bend * bend) * (root * (1.0 + 3.0 * cube * square))
    hidden_ref[...] = (act * upper).astype(jnp.bfloat16)
    grad_gate = (grad_hidden * upper * slope).astype(jnp.bfloat16)
    grad_upper = (grad_hidden * act).astype(jnp.bfloat16)
    grad_ref[:, pl.ds(pl.multiple_of(step * size, size), size)] = grad_gate
    grad_ref[:, pl.ds(pl.multiple_of(inner + step * size, size), size)] = grad_upper


def feed(normed, grad_hidden, weights):
    group, width = normed.shape
    inner = grad_hidden.shape[1]
    steps = inner // FBLOCK
    whole = lambda n: pl.BlockSpec((group, n), lambda i: (0, 0))
    columns = pl.BlockSpec((group, FBLOCK), lambda i: (0, i))
    return pl.pallas_call(
        feed_kernel,
        grid=(steps,),
        in_specs=[
            whole(width),
            columns,
            pl.BlockSpec((width, FBLOCK), lambda i: (0, i)),
            pl.BlockSpec((width, FBLOCK), lambda i: (0, steps + i)),
        ],
        out_specs=[columns, whole(2 * inner)],
        out_shape=[
            jax.ShapeDtypeStruct((group, inner), jnp.bfloat16),
            jax.ShapeDtypeStruct((group, 2 * inner), jnp.bfloat16),
        ],
        compiler_params=pltpu.CompilerParams(vmem_limit_bytes=48 * 1024 * 1024),
        name="feed",
    )(normed, grad_hidden, weights, weights)


def back_kernel(left_ref, right_ref, out_ref):
    out_ref[...] = inner_cols(left_ref[...], right_ref[...]).astype(jnp.bfloat16)


def back(left, right):
    rows, inner = left.shape
    columns = right.shape[0]
    size = 2 * BLOCK
    return pl.pallas_call(
        back_kernel,
        grid=(columns // size,),
        in_specs=[
            pl.BlockSpec((rows, inner), lambda i: (0, 0)),
            pl.BlockSpec((size, inner), lambda i: (i, 0)),
        ],
        out_specs=pl.BlockSpec((rows, size), lambda i: (0, i)),
        out_shape=jax.ShapeDtypeStruct((rows, columns), jnp.bfloat16),
        compiler_params=pltpu.CompilerParams(vmem_limit_bytes=40 * 1024 * 1024),
        name="back",
    )(left, right)


def outer_kernel(left_ref, right_ref, out_ref):
    out_ref[...] = inner_rows(left_ref[...], right_ref[...]).astype(jnp.bfloat16)


def outer(left, right):
    rows, wide = left.shape
    columns = right.shape[1]
    size = 2 * BLOCK
    return pl.pallas_call(
        outer_kernel,
        grid=(wide // size,),
        in_specs=[
            pl.BlockSpec((rows, size), lambda i: (0, i)),
            pl.BlockSpec((rows, columns), lambda i: (0, 0)),
        ],
        out_specs=pl.BlockSpec((size, columns), lambda i: (i, 0)),
        out_shape=pltpu.HBM((wide, columns), jnp.bfloat16),
        compiler_params=pltpu.CompilerParams(vmem_limit_bytes=40 * 1024 * 1024),
        name="outer",
    )(left, right)


def times_kernel(left_ref, right_ref, out_ref):
    out_ref[...] = jnp.dot(
        left_ref[...], right_ref[...], preferred_element_type=jnp.float32
    ).astype(jnp.bfloat16)


def times(left, right):
    rows, inner = left.shape
    columns = right.shape[1]
    size = 4 * BLOCK
    return pl.pallas_call(
        times_kernel,
        grid=(columns // size,),
        in_specs=[
            pl.BlockSpec((rows, inner), lambda i: (0, 0)),
            pl.BlockSpec((inner, size), lambda i: (0, i)),
        ],
        out_specs=pl.BlockSpec((rows, size), lambda i: (0, i)),
        out_shape=jax.ShapeDtypeStruct((rows, columns), jnp.bfloat16),
        compiler_params=pltpu.CompilerParams(vmem_limit_bytes=40 * 1024 * 1024),
        name="times",
    )(left, right)


def shards(
    tokens,
    seq_lengths,
    seq_order,
    norm_gain,
    query_weight,
    key_value_weight,
    out_weight,
    mlp_gain,
    gate_weight,
    up_weight,
    down_weight,
    cotangent,
):
    rows = tokens.shape[2]
    width = tokens.shape[3]
    group_rows = rows * RING
    q_cols = HEADS // RING * HD
    f_cols = gate_weight.shape[1] // RING
    own_rows = query_weight.shape[0]
    shard_index = lax.axis_index("shard")
    seq_index = lax.axis_index("seq")
    grp_index = lax.axis_index("grp")
    own_tokens = tokens[0, 0]
    own_cotangent = cotangent[0, 0]

    gains = jnp.pad(jnp.stack([norm_gain, mlp_gain], axis=1), ((0, 0), (0, HD - 2)))

    def pick_q(i):
        own = lax.dynamic_slice_in_dim(query_weight, i * q_cols, q_cols, 1)
        return jnp.concatenate([own, key_value_weight, gains], axis=1)

    def pick_f(i):
        return jnp.concatenate(
            [
                lax.dynamic_slice_in_dim(gate_weight, i * f_cols, f_cols, 1),
                lax.dynamic_slice_in_dim(up_weight, i * f_cols, f_cols, 1),
            ],
            axis=1,
        )

    group_start = shard_index * group_rows
    ring_rows = (seq_index + jnp.arange(RING, dtype=jnp.int32)) % RING * rows
    in_group = (ring_rows[:, None] + jnp.arange(rows, dtype=jnp.int32)[None, :]).reshape(-1)
    query_index = group_start + in_group
    starts = slot_starts(seq_lengths[0], seq_order[0])
    begins = jnp.max(
        jnp.where(query_index[:, None] >= starts[None, :], starts[None, :], 0), axis=1
    )
    cos, sin = rotation(query_index - begins)
    info = jnp.concatenate([jnp.stack([shard_index, seq_index]).astype(jnp.int32), starts])

    def scattered(grad, dim):
        return lax.psum_scatter(grad, "shard", scatter_dimension=dim, tiled=True)

    w_out = lax.all_gather(out_weight, "shard", axis=0, tiled=True)
    got = exchange_parts(pick_q, "seq", seq_index)
    tok_after = send(own_tokens, "seq", -1)
    tok_before = send(own_tokens, "seq", 1)
    *got, tok_after, tok_before, gate_weight, up_weight, down_weight = fence(
        *got, tok_after, tok_before, gate_weight, up_weight, down_weight
    )
    w_down = lax.all_gather(down_weight, "shard", axis=0, tiled=True)
    block = jnp.stack(got)
    block_after = send_x(block, -1)
    block_before = send_x(block, 1)
    half = rows // 2
    tok_far_a = send(tok_after[:half], "seq", -1)
    tok_far_b = send(tok_before[half:], "seq", 1)
    block_after, block_before, tok_far_a, tok_far_b, gate_weight, up_weight, w_out = fence(
        block_after, block_before, tok_far_a, tok_far_b, gate_weight, up_weight, w_out
    )
    block_far_a = send_x(block_after[: RING // 2], -1)
    block_far_b = send_x(block_before[RING // 2 :], 1)
    near = send_core(jnp.stack([block, block_after, block_before]))
    got = exchange_parts(pick_f, "seq", seq_index)
    tokens_bf = jnp.concatenate([own_tokens, tok_after, tok_far_a, tok_far_b, tok_before], axis=0)
    block_far_a, block_far_b, near, tokens_bf = fence(block_far_a, block_far_b, near, tokens_bf)
    far = send_core(jnp.concatenate([block_far_a, block_far_b]))
    pieces = (block, block_after, block_far_a, block_far_b, block_before, near, far)
    normed_one, queries, pair, scale_one, gain_rows, w_attn = project(
        info, tokens_bf, cos, sin, pieces
    )
    kvs = [shifted(pair, "shard", 2), shifted(pair, "shard", 1), pair]
    *got, own_cotangent = fence(*got, *kvs, own_cotangent)
    got, kvs = got[:RING], got[RING:]
    w_ff = lax.all_gather(by_source(got, seq_index), "shard", axis=1, tiled=True)
    w_ff = w_ff.reshape(width, -1)
    cot_after = send(own_cotangent, "seq", -1)
    cot_before = send(own_cotangent, "seq", 1)
    gain_one, gain_two = gain_rows[0], gain_rows[1]
    attended, lse = attend(info, queries, kvs)
    attended, cot_after, cot_before, w_down = fence(attended, cot_after, cot_before, w_down)
    cot_far_a = send(cot_after[:half], "seq", -1)
    cot_far_b = send(cot_before[half:], "seq", 1)
    all_cotangent = jnp.concatenate(
        [own_cotangent, cot_after, cot_far_a, cot_far_b, cot_before], axis=0
    )

    branch = scatter_ring(row_blocks(matmul(attended, w_out)), "seq")
    middle = own_tokens.astype(jnp.float32) + branch
    scale_two = norm_scale(middle)
    normed_two = (middle * scale_two * gain_two).astype(jnp.bfloat16)
    n_after = send(normed_two, "seq", -1)
    n_before = send(normed_two, "seq", 1)
    normed_two, n_after, n_before = fence(normed_two, n_after, n_before)
    n_far_a = send(n_after[:half], "seq", -1)
    n_far_b = send(n_before[half:], "seq", 1)
    normed_two = jnp.concatenate([normed_two, n_after, n_far_a, n_far_b, n_before], axis=0)
    grad_hidden, normed_two = fence(inner_cols(all_cotangent, w_down), normed_two)
    hidden, grad_ff = feed(normed_two, grad_hidden, w_ff)
    grad_down = outer(hidden, all_cotangent)
    share_down = scattered(grad_down, 0)
    grad_down, grad_ff = fence(grad_down, grad_ff)
    partial_two = back(grad_ff, w_ff)
    part = own_rows // RING

    def first_half(parts):
        return send(parts[2][:half], "seq", 1), send(parts[2][half:], "seq", -1)

    def second_half(parts, got_a, got_b):
        one, last = [parts[i].astype(jnp.float32) for i in (1, 3)]
        one = jnp.concatenate([one[:half] + got_a.astype(jnp.float32), one[half:]], axis=0)
        last = jnp.concatenate([last[:half], last[half:] + got_b.astype(jnp.float32)], axis=0)
        return (
            send(one.astype(jnp.bfloat16), "seq", 1),
            send(last.astype(jnp.bfloat16), "seq", -1),
        )

    def total(*blocks):
        return sum(block.astype(jnp.float32) for block in blocks)

    parts = row_blocks(partial_two)
    two_a, two_b = first_half(parts)
    two_a, two_b, grad_ff = fence(two_a, two_b, grad_ff)
    from_last, from_next = second_half(parts, two_a, two_b)
    grad_wff = outer(normed_two, grad_ff)
    from_last, from_next, grad_wff, hidden = fence(from_last, from_next, grad_wff, hidden)
    share_ff = scattered(grad_wff.reshape(RING, -1, 2 * f_cols), 1)
    grad_normed_two = total(parts[0], from_last, from_next)
    grad_middle = own_cotangent.astype(jnp.float32) + norm_back(
        middle, scale_two, gain_two, grad_normed_two
    )
    own_branch = grad_middle.astype(jnp.bfloat16)

    gb_after = send(own_branch, "seq", -1)
    gb_before = send(own_branch, "seq", 1)
    out_parts = times(hidden, w_down)
    gb_after, gb_before, out_parts, own_branch, share_down = fence(
        gb_after, gb_before, out_parts, own_branch, share_down
    )
    gb_far_a = send(gb_after[:half], "seq", -1)
    gb_far_b = send(gb_before[half:], "seq", 1)
    gb_far_a, gb_far_b, share_down = fence(gb_far_a, gb_far_b, share_down)
    grad_branch = jnp.concatenate([own_branch, gb_after, gb_far_a, gb_far_b, gb_before], axis=0)
    grad_attended = inner_cols(grad_branch, w_out).astype(jnp.bfloat16)

    down_pieces = exchange_parts(
        lambda i: lax.dynamic_index_in_dim(
            share_down.reshape(RING, -1, width), i, 0, keepdims=False
        ),
        "grp",
        grp_index,
    )
    grad_queries, grad_table = attend_back(info, queries, grad_attended, lse, cos, sin, kvs)
    grad_queries, grad_table, *down_pieces = fence(grad_queries, grad_table, *down_pieces)

    returned_two = shifted(grad_table[0].astype(jnp.bfloat16), "shard", -2)
    returned_one = shifted(grad_table[1].astype(jnp.bfloat16), "shard", -1)

    def grp_pieces(share, dim):
        return exchange_parts(
            lambda i: lax.dynamic_index_in_dim(share, i, dim, keepdims=False), "grp", grp_index
        )

    def seq_pieces(summed):
        return exchange_parts(
            lambda i: lax.dynamic_index_in_dim(summed, i, 0, keepdims=False), "seq", seq_index
        )

    def side_by_side(columns):
        return columns.transpose(1, 0, 2).reshape(columns.shape[1], -1)

    returned_one, returned_two, grad_table, *down_pieces = fence(
        returned_one, returned_two, grad_table, *down_pieces
    )
    grad_pair = total(grad_table[2], returned_one, returned_two)
    grad_keys = grad_pair[:, :HD]
    swapped = jnp.concatenate([grad_keys[:, HD // 2 :], grad_keys[:, : HD // 2]], axis=1)
    grad_keys = grad_keys * cos - swapped * sin
    grad_pair = jnp.concatenate([grad_keys, grad_pair[:, HD:]], axis=1).astype(jnp.bfloat16)
    gain_two_terms = (grad_normed_two * middle * scale_two).astype(jnp.bfloat16)
    partial_one, grad_attn = unproject(
        grad_queries, grad_pair, w_attn, normed_one, tokens_bf, scale_one, attended, grad_branch,
        gain_two_terms,
    )
    parts = row_blocks(partial_one)
    one_a, one_b = first_half(parts)
    n_attn = w_attn.shape[1]
    share_attn = scattered(grad_attn.reshape(RING, -1, grad_attn.shape[1]), 1)
    one_a, one_b, share_ff, *down_pieces = fence(one_a, one_b, share_ff, *down_pieces)
    from_last, from_next = second_half(parts, one_a, one_b)
    ff_pieces = grp_pieces(share_ff.reshape(RING, RING, part, -1), 1)
    from_last, from_next, *ff_pieces = fence(from_last, from_next, *ff_pieces)
    ff_pieces = seq_pieces(total(*ff_pieces).astype(jnp.bfloat16))
    down_own = total(*down_pieces).astype(jnp.bfloat16)
    down_got = [send(down_own, "grp", -k) for k in range(1, RING)]
    down_got, ff_pieces = fence(down_got, ff_pieces)
    share_down = ordered([down_own] + down_got, grp_index).reshape(-1, width)
    share_down = share_down.astype(jnp.float32)
    ff_columns = by_source(ff_pieces, seq_index)
    ff_rows = jnp.concatenate(
        [side_by_side(ff_columns[:, :, :f_cols]), side_by_side(ff_columns[:, :, f_cols:])], axis=1
    )
    ff_after = send(ff_rows, "grp", -1)
    ff_before = send(ff_rows, "grp", 1)
    grad_normed_one = total(parts[0], from_last, from_next)
    own_inputs = own_tokens.astype(jnp.float32)
    input_grad = grad_middle + norm_back(
        own_inputs, norm_scale(own_inputs), gain_one, grad_normed_one
    )
    ff_after, ff_before, input_grad = fence(ff_after, ff_before, input_grad)
    ff_far_a = send(ff_after[: part // 2], "grp", -1)
    ff_far_b = send(ff_before[part // 2 :], "grp", 1)
    out_whole = ordered(row_blocks(out_parts), seq_index).reshape(group_rows, width)
    ff_far_a, ff_far_b, share_attn, out_whole = fence(ff_far_a, ff_far_b, share_attn, out_whole)
    out_own = lax.psum_scatter(out_whole, "seq", scatter_dimension=0, tiled=True)
    layer_output = (middle + out_own.astype(jnp.float32)).astype(jnp.bfloat16)[None, None]
    pieces = grp_pieces(share_attn.reshape(RING, RING, part, -1), 1)
    ff_far = jnp.concatenate([ff_far_a, ff_far_b], axis=0)
    ff_rows = ordered([ff_rows, ff_after, ff_far, ff_before], grp_index)
    ff_rows = ff_rows.reshape(own_rows, -1).astype(jnp.float32)
    share_gate = ff_rows[:, : RING * f_cols]
    share_upper = ff_rows[:, RING * f_cols :]
    summed = total(*pieces).astype(jnp.bfloat16)
    out_own = side_by_side(summed[:, :, n_attn:])
    columns = by_source(seq_pieces(summed[:, :, :n_attn]), seq_index)
    summed = total(*[columns[i, :, q_cols:] for i in range(RING)]).astype(jnp.bfloat16)
    attn_rows = jnp.concatenate(
        [side_by_side(columns[:, :, :q_cols]), out_own, summed], axis=1
    )
    attn_rows = gather_direct(attn_rows, "grp", grp_index).reshape(own_rows, -1)
    attn_rows = attn_rows.astype(jnp.float32)
    share_query = attn_rows[:, :width]
    share_out = attn_rows[:, width : 2 * width]
    share_pair = attn_rows[:, 2 * width : 2 * width + 2 * HD]
    share_gain_one = attn_rows[:, 2 * width + 2 * HD]
    share_gain_two = attn_rows[:, 2 * width + 2 * HD + 1]
    return (
        layer_output,
        input_grad[None, None],
        share_gain_one,
        share_query,
        share_pair,
        share_out,
        share_gain_two,
        share_gate,
        share_upper,
        share_down,
    )


def solution(mesh):
    by_row = P(("seq", "shard"), None)
    by_entry = P(("seq", "shard"))
    by_token = P("grp", "shard", "seq", None)
    return jax.shard_map(
        shards,
        mesh=mesh,
        in_specs=(
            by_token,
            P("grp", None),
            P("grp", None),
            by_entry,
            by_row,
            by_row,
            by_row,
            by_entry,
            by_row,
            by_row,
            by_row,
            by_token,
        ),
        out_specs=(
            by_token,
            by_token,
            by_entry,
            by_row,
            by_row,
            by_row,
            by_entry,
            by_row,
            by_row,
            by_row,
        ),
        check_vma=False,
    )
```

```python
import functools

import jax
import jax.numpy as jnp
from jax import lax
from jax.experimental import pallas as pl
from jax.experimental.pallas import tpu as pltpu
from jax.sharding import PartitionSpec as P

HEADS = 16
HD = 128
WINDOW = 1024
RING = 4
BLOCK = 128
CHUNK = 32
FBLOCK = 512

epsilon = 1e-06
big_negative = -1e30


def send(value, axis, steps):
    count = lax.axis_size(axis)
    return lax.ppermute(value, axis, [(i, (i + steps) % count) for i in range(count)])


def send_x(value, steps):
    return lax.ppermute(
        value,
        "shard",
        [(x * 2 + c, (x + steps) % RING * 2 + c) for x in range(RING) for c in range(2)],
    )


def send_core(value):
    return lax.ppermute(
        value, "shard", [(x * 2 + c, x * 2 + 1 - c) for x in range(RING) for c in range(2)]
    )


def fence(*values):
    return lax.optimization_barrier(values)


def shifted(value, axis, steps):
    count = lax.axis_size(axis)
    initial, last = (max(0, -steps), min(count, count - steps))
    return lax.ppermute(value, axis, [(i, i + steps) for i in range(initial, last)])


def scatter_ring(parts, axis):
    far = parts[2]
    own, nxt, prv = [parts[i].astype(jnp.float32) for i in (0, 1, 3)]
    half = own.shape[0] // 2
    got_a = send(far[:half].astype(jnp.bfloat16), axis, 1).astype(jnp.float32)
    got_b = send(far[half:].astype(jnp.bfloat16), axis, -1).astype(jnp.float32)
    nxt = jnp.concatenate([nxt[:half] + got_a, nxt[half:]], axis=0)
    prv = jnp.concatenate([prv[:half], prv[half:] + got_b], axis=0)
    from_prv = send(nxt.astype(jnp.bfloat16), axis, 1).astype(jnp.float32)
    from_nxt = send(prv.astype(jnp.bfloat16), axis, -1).astype(jnp.float32)
    return own + from_prv + from_nxt


def ordered(parts, index):
    return jnp.stack(
        [
            lax.select_n(index, *[parts[(place - m) % RING] for m in range(RING)])
            for place in range(RING)
        ],
        axis=0,
    )


def exchange_parts(pick, axis, index):
    got = [pick((index + k) % RING) for k in range(RING)]
    return [got[0]] + [send(got[k], axis, k) for k in range(1, RING)]


def by_source(got, index):
    return ordered([got[0], got[3], got[2], got[1]], index)


def exchange(pick, axis, index):
    return by_source(exchange_parts(pick, axis, index), index)


def row_blocks(total):
    rows = total.shape[0] // RING
    return [total[i * rows : (i + 1) * rows] for i in range(RING)]


def norm_scale(values):
    return lax.rsqrt(jnp.mean(values * values, axis=-1, keepdims=True) + epsilon)


def norm_back(values, scale, gain, grad):
    scaled = grad * gain
    dot = jnp.mean(scaled * values, axis=-1, keepdims=True)
    return scaled * scale - values * (scale * scale * scale * dot)


def slot_starts(lengths, packing):
    slots = jnp.arange(lengths.shape[0], dtype=jnp.int32)
    picked = (packing[:, None] == slots[None, :]).astype(jnp.int32)
    packed = jnp.sum(picked * lengths[None, :], axis=1, dtype=jnp.int32)
    return jnp.cumsum(packed, dtype=jnp.int32) - packed


def rotation(place):
    half_width = HD // 2
    frequency = 10000.0 ** (-jnp.arange(half_width, dtype=jnp.float32) / half_width)
    angle = place.astype(jnp.float32)[:, None] * frequency
    cosine, sine = jnp.cos(angle), jnp.sin(angle)
    return jnp.concatenate([cosine, cosine], axis=1), jnp.concatenate([-sine, sine], axis=1)


def matmul(left, right):
    return jnp.dot(left, right, preferred_element_type=jnp.float32)


def inner_rows(left, right):
    return lax.dot_general(
        left, right, (((0,), (0,)), ((), ())), preferred_element_type=jnp.float32
    )


def inner_cols(left, right):
    return lax.dot_general(
        left, right, (((1,), (1,)), ((), ())), preferred_element_type=jnp.float32
    )


def tile_mask(info, tile, first_row, rows, reach, group):
    shard, seq = info[0], info[1]
    base = shard * group
    row = lax.broadcasted_iota(jnp.int32, (rows, 1), 0) + first_row
    query = base + (seq + tile) % RING * BLOCK + row
    begin = jnp.zeros_like(query)
    for slot in range(info.shape[0] - 2):
        start = info[2 + slot]
        begin = jnp.where(query >= start, jnp.maximum(begin, start), begin)
    lowest = jnp.maximum(begin, query - (WINDOW - 1))
    lane = lax.broadcasted_iota(jnp.int32, (1, reach), 1)
    block = lane // group
    in_block = lane - block * group
    key = base + (block - (reach // group - 1)) * group
    key = key + (seq + in_block // BLOCK) % RING * BLOCK + in_block % BLOCK
    return (key <= query) & (key >= lowest)


def attend_kernel(info, q_ref, *refs, heads, group):
    kv_refs, (out_ref, lse_ref, scores_ref, soft_ref) = refs[:-4], refs[-4:]
    reach = group * len(kv_refs)
    tile = pl.program_id(0)
    q = jnp.concatenate([q_ref[:, h * HD : (h + 1) * HD] for h in range(heads)], axis=0)
    for b, kv in enumerate(kv_refs):
        scores_ref[:, b * group : (b + 1) * group] = inner_cols(q, kv[:, :HD])
    for part in range(BLOCK // CHUNK):
        mask = tile_mask(info, tile, part * CHUNK, CHUNK, reach, group)
        for h in range(heads):
            at = pl.ds(h * BLOCK + part * CHUNK, CHUNK)
            scores = jnp.where(mask, scores_ref[at, :] * (HD**-0.5), big_negative)
            top = jnp.max(scores, axis=1, keepdims=True)
            expo = jnp.exp(scores - top)
            total = jnp.sum(expo, axis=1, keepdims=True)
            soft_ref[at, :] = (expo * (1.0 / total)).astype(jnp.bfloat16)
            lse_ref[0, at, :] = jnp.broadcast_to(top + jnp.log(total), (CHUNK, HD))
    acc = None
    for b, kv in enumerate(kv_refs):
        term = jnp.dot(soft_ref[:, b * group : (b + 1) * group], kv[:, HD:], preferred_element_type=jnp.float32)
        acc = term if acc is None else acc + term
    for h in range(heads):
        out_ref[:, h * HD : (h + 1) * HD] = acc[h * BLOCK : (h + 1) * BLOCK].astype(jnp.bfloat16)


def attend(info, queries, kvs):
    group, width = queries.shape
    heads = width // HD
    reach = group * len(kvs)
    whole = pl.BlockSpec((group, 2 * HD), lambda i: (0, 0))
    rows = pl.BlockSpec((BLOCK, width), lambda i: (i, 0))
    return pl.pallas_call(
        functools.partial(attend_kernel, heads=heads, group=group),
        grid=(group // BLOCK,),
        in_specs=[pl.BlockSpec(memory_space=pltpu.SMEM), rows] + [whole] * len(kvs),
        out_specs=[rows, pl.BlockSpec((1, heads * BLOCK, HD), lambda i: (i, 0, 0))],
        out_shape=[
            jax.ShapeDtypeStruct((group, width), jnp.bfloat16),
            jax.ShapeDtypeStruct((group // BLOCK, heads * BLOCK, HD), jnp.float32),
        ],
        scratch_shapes=[
            pltpu.VMEM((heads * BLOCK, reach), jnp.float32),
            pltpu.VMEM((heads * BLOCK, reach), jnp.bfloat16),
        ],
        compiler_params=pltpu.CompilerParams(vmem_limit_bytes=40 * 1024 * 1024),
        name="attend",
    )(info, queries, *kvs)


def attend_back_kernel(info, q_ref, do_ref, lse_ref, cos_ref, sin_ref, *refs, heads, group):
    count = len(refs) - 6
    kv_refs, (dq_ref, dkv_ref, scores_ref, dsoft_ref, soft_ref, dscores_ref) = refs[:count], refs[count:]
    reach = group * count
    tile = pl.program_id(0)

    @pl.when(tile == 0)
    def _():
        dkv_ref[...] = jnp.zeros_like(dkv_ref)

    q = jnp.concatenate([q_ref[:, h * HD : (h + 1) * HD] for h in range(heads)], axis=0)
    do = jnp.concatenate([do_ref[:, h * HD : (h + 1) * HD] for h in range(heads)], axis=0)
    for b, kv in enumerate(kv_refs):
        at = slice(b * group, (b + 1) * group)
        scores_ref[:, at] = inner_cols(q, kv[:, :HD])
        dsoft_ref[:, at] = inner_cols(do, kv[:, HD:])
    for part in range(BLOCK // CHUNK):
        mask = tile_mask(info, tile, part * CHUNK, CHUNK, reach, group)
        for h in range(heads):
            at = pl.ds(h * BLOCK + part * CHUNK, CHUNK)
            lse = lse_ref[0, at, 0:1]
            scores = jnp.where(mask, scores_ref[at, :] * (HD**-0.5), big_negative)
            soft = jnp.exp(scores - lse)
            dsoft = dsoft_ref[at, :]
            delta = jnp.sum(soft * dsoft, axis=1, keepdims=True)
            soft_ref[at, :] = soft.astype(jnp.bfloat16)
            dscores_ref[at, :] = (soft * (dsoft - delta)).astype(jnp.bfloat16)
    dq = None
    for b, kv in enumerate(kv_refs):
        at = slice(b * group, (b + 1) * group)
        term = jnp.dot(dscores_ref[:, at], kv[:, :HD], preferred_element_type=jnp.float32)
        dq = term if dq is None else dq + term
        dkv_ref[b, :, :HD] += inner_rows(dscores_ref[:, at], q) * (HD**-0.5)
        dkv_ref[b, :, HD:] += inner_rows(soft_ref[:, at], do)
    cos, sin = cos_ref[...], sin_ref[...]
    for h in range(heads):
        one = dq[h * BLOCK : (h + 1) * BLOCK] * (HD**-0.5)
        one = one * cos - pltpu.roll(one, HD // 2, 1) * sin
        dq_ref[:, h * HD : (h + 1) * HD] = one.astype(jnp.bfloat16)


def attend_back(info, queries, grads, lse, cos, sin, kvs):
    group, width = queries.shape
    heads = width // HD
    reach = group * len(kvs)
    whole = pl.BlockSpec((group, 2 * HD), lambda i: (0, 0))
    rows = pl.BlockSpec((BLOCK, width), lambda i: (i, 0))
    table = pl.BlockSpec((BLOCK, HD), lambda i: (i, 0))
    return pl.pallas_call(
        functools.partial(attend_back_kernel, heads=heads, group=group),
        grid=(group // BLOCK,),
        in_specs=[
            pl.BlockSpec(memory_space=pltpu.SMEM),
            rows,
            rows,
            pl.BlockSpec((1, heads * BLOCK, HD), lambda i: (i, 0, 0)),
            table,
            table,
        ]
        + [whole] * len(kvs),
        out_specs=[rows, pl.BlockSpec((len(kvs), group, 2 * HD), lambda i: (0, 0, 0))],
        out_shape=[
            jax.ShapeDtypeStruct((group, width), jnp.bfloat16),
            jax.ShapeDtypeStruct((len(kvs), group, 2 * HD), jnp.float32),
        ],
        scratch_shapes=[
            pltpu.VMEM((heads * BLOCK, reach), jnp.float32),
            pltpu.VMEM((heads * BLOCK, reach), jnp.float32),
            pltpu.VMEM((heads * BLOCK, reach), jnp.bfloat16),
            pltpu.VMEM((heads * BLOCK, reach), jnp.bfloat16),
        ],
        compiler_params=pltpu.CompilerParams(vmem_limit_bytes=40 * 1024 * 1024),
        name="attend_back",
    )(info, queries, grads, lse, cos, sin, *kvs)


def project_kernel(
    info, tok_ref, cos_ref, sin_ref, own, after, far_a, far_b, before, near, far,
    n_ref, q_ref, kv_ref, scale_ref, gains_ref, w_ref, sems, *, heads, block
):
    q_cols = heads * HD

    @pl.when(pl.program_id(0) == 0)
    def _():
        x, core, seq = info[0] // 2, info[0] % 2, info[1]
        copies = []

        def fetch(piece, k, other, first):
            place = (x + k) % RING * 2 + (1 - core if other else core)
            for i in range(piece.shape[0]):
                source = (seq - first - i + RING) % RING
                at = pl.multiple_of(source * 8 * block + place * block, block)
                copies.append(
                    pltpu.make_async_copy(
                        piece.at[i], w_ref.at[pl.ds(at, block), :], sems.at[len(copies)]
                    )
                )

        half = RING // 2
        fetch(own, 0, False, 0)
        fetch(after, 1, False, 0)
        fetch(far_a, 2, False, 0)
        fetch(far_b, 2, False, half)
        fetch(before, 3, False, 0)
        fetch(near.at[0], 0, True, 0)
        fetch(near.at[1], 1, True, 0)
        fetch(far, 2, True, 0)
        fetch(near.at[2], 3, True, 0)
        for copy in copies:
            copy.start()
        for copy in copies:
            copy.wait()
        pick = lax.broadcasted_iota(jnp.int32, (8, HD), 0) == lax.broadcasted_iota(
            jnp.int32, (8, HD), 1
        )
        gains_ref[...] = inner_cols(pick.astype(jnp.bfloat16), w_ref[:, q_cols + 2 * HD :])

    x = tok_ref[...].astype(jnp.float32)
    scale = lax.rsqrt(jnp.mean(x * x, axis=1, keepdims=True) + epsilon)
    normed = (x * scale * gains_ref[0:1, :]).astype(jnp.bfloat16)
    n_ref[...] = normed
    scale_ref[...] = jnp.broadcast_to(scale, scale_ref.shape)
    qkv = jnp.dot(normed, w_ref[:, : q_cols + 2 * HD], preferred_element_type=jnp.float32)
    cos, sin = cos_ref[...], sin_ref[...]
    for h in range(heads + 1):
        one = qkv[:, h * HD : (h + 1) * HD]
        one = (one * cos + pltpu.roll(one, HD // 2, 1) * sin).astype(jnp.bfloat16)
        if h < heads:
            q_ref[:, h * HD : (h + 1) * HD] = one
        else:
            kv_ref[:, :HD] = one
    kv_ref[:, HD:] = qkv[:, (heads + 1) * HD :].astype(jnp.bfloat16)


def project(info, tokens, cos, sin, pieces):
    group, width = tokens.shape
    block, columns = pieces[0].shape[1:]
    heads = columns // HD - 3
    rows = lambda n: pl.BlockSpec((BLOCK, n), lambda i: (i, 0))
    whole = lambda shape: pl.BlockSpec(shape, lambda i: (0, 0))
    return pl.pallas_call(
        functools.partial(project_kernel, heads=heads, block=block),
        grid=(group // BLOCK,),
        in_specs=[pl.BlockSpec(memory_space=pltpu.SMEM), rows(width), rows(HD), rows(HD)]
        + [pl.BlockSpec(memory_space=pl.ANY)] * len(pieces),
        out_specs=[
            rows(width),
            rows(heads * HD),
            rows(2 * HD),
            rows(HD),
            whole((8, width)),
            whole((width, columns)),
        ],
        out_shape=[
            jax.ShapeDtypeStruct((group, width), jnp.bfloat16),
            jax.ShapeDtypeStruct((group, heads * HD), jnp.bfloat16),
            jax.ShapeDtypeStruct((group, 2 * HD), jnp.bfloat16),
            jax.ShapeDtypeStruct((group, HD), jnp.float32),
            jax.ShapeDtypeStruct((8, width), jnp.float32),
            jax.ShapeDtypeStruct((width, columns), jnp.bfloat16),
        ],
        scratch_shapes=[pltpu.SemaphoreType.DMA((8 * RING,))],
        compiler_params=pltpu.CompilerParams(vmem_limit_bytes=40 * 1024 * 1024),
        name="project",
    )(info, tokens, cos, sin, *pieces)


def unproject_kernel(
    dq_ref, dkv_ref, w_ref, n_ref, tok_ref, scale_ref, att_ref, branch_ref, two_ref,
    part_ref, grad_ref
):
    q_cols = dq_ref.shape[1]
    n_attn = w_ref.shape[1]
    grads = jnp.concatenate([dq_ref[...], dkv_ref[...]], axis=1)
    part = inner_cols(grads, w_ref[:, : q_cols + 2 * HD])
    part_ref[...] = part.astype(jnp.bfloat16)
    terms = (part * tok_ref[...].astype(jnp.float32) * scale_ref[:, 0:1]).astype(jnp.bfloat16)
    column = lax.broadcasted_iota(jnp.int32, (part.shape[0], HD), 1)
    first = (column == 0).astype(jnp.bfloat16)
    second = (column == 1).astype(jnp.bfloat16)[: two_ref.shape[0]]
    grad_ref[:, : q_cols + 2 * HD] = inner_rows(n_ref[...], grads).astype(jnp.bfloat16)
    gains = inner_rows(terms, first) + inner_rows(two_ref[...], second)
    grad_ref[:, q_cols + 2 * HD : n_attn] = gains.astype(jnp.bfloat16)
    grad_ref[:, n_attn:] = inner_rows(att_ref[...], branch_ref[...]).astype(jnp.bfloat16)


def unproject(
    grad_queries, grad_pair, weights, normed, tokens, scale, attended, grad_branch, two
):
    group, width = tokens.shape
    size = 4 * BLOCK
    columns = weights.shape[1]
    whole = lambda n: pl.BlockSpec((group, n), lambda i: (0, 0))
    across = pl.BlockSpec((group, size), lambda i: (0, i))
    down = pl.BlockSpec((size, columns), lambda i: (i, 0))
    return pl.pallas_call(
        unproject_kernel,
        grid=(width // size,),
        in_specs=[
            whole(grad_queries.shape[1]),
            whole(grad_pair.shape[1]),
            down,
            across,
            across,
            whole(HD),
            whole(attended.shape[1]),
            across,
            pl.BlockSpec((two.shape[0], size), lambda i: (0, i)),
        ],
        out_specs=[across, pl.BlockSpec((size, columns + size), lambda i: (i, 0))],
        out_shape=[
            jax.ShapeDtypeStruct((group, width), jnp.bfloat16),
            jax.ShapeDtypeStruct((width, columns + size), jnp.bfloat16),
        ],
        compiler_params=pltpu.CompilerParams(vmem_limit_bytes=40 * 1024 * 1024),
        name="unproject",
    )(grad_queries, grad_pair, weights, normed, tokens, scale, attended, grad_branch, two)


def feed_kernel(n_ref, gh_ref, gate_ref, up_ref, hidden_ref, grad_ref):
    step = pl.program_id(0)
    size = gate_ref.shape[1]
    inner = grad_ref.shape[1] // 2
    gate = jnp.dot(n_ref[...], gate_ref[...], preferred_element_type=jnp.float32)
    upper = jnp.dot(n_ref[...], up_ref[...], preferred_element_type=jnp.float32)
    grad_hidden = gh_ref[...]
    root, cube = 0.7978845608028654, 0.044715
    square = gate * gate
    bend = jnp.tanh(root * gate * (1.0 + cube * square))
    half = 0.5 * (1.0 + bend)
    act = gate * half
    slope = half + 0.5 * gate * (1.0 - bend * bend) * (root * (1.0 + 3.0 * cube * square))
    hidden_ref[...] = (act * upper).astype(jnp.bfloat16)
    grad_gate = (grad_hidden * upper * slope).astype(jnp.bfloat16)
    grad_upper = (grad_hidden * act).astype(jnp.bfloat16)
    grad_ref[:, pl.ds(pl.multiple_of(step * size, size), size)] = grad_gate
    grad_ref[:, pl.ds(pl.multiple_of(inner + step * size, size), size)] = grad_upper


def feed(normed, grad_hidden, weights):
    group, width = normed.shape
    inner = grad_hidden.shape[1]
    steps = inner // FBLOCK
    whole = lambda n: pl.BlockSpec((group, n), lambda i: (0, 0))
    columns = pl.BlockSpec((group, FBLOCK), lambda i: (0, i))
    return pl.pallas_call(
        feed_kernel,
        grid=(steps,),
        in_specs=[
            whole(width),
            columns,
            pl.BlockSpec((width, FBLOCK), lambda i: (0, i)),
            pl.BlockSpec((width, FBLOCK), lambda i: (0, steps + i)),
        ],
        out_specs=[columns, whole(2 * inner)],
        out_shape=[
            jax.ShapeDtypeStruct((group, inner), jnp.bfloat16),
            jax.ShapeDtypeStruct((group, 2 * inner), jnp.bfloat16),
        ],
        compiler_params=pltpu.CompilerParams(vmem_limit_bytes=48 * 1024 * 1024),
        name="feed",
    )(normed, grad_hidden, weights, weights)


def back_kernel(left_ref, right_ref, out_ref):
    out_ref[...] = inner_cols(left_ref[...], right_ref[...]).astype(jnp.bfloat16)


def back(left, right):
    rows, inner = left.shape
    columns = right.shape[0]
    size = 2 * BLOCK
    return pl.pallas_call(
        back_kernel,
        grid=(columns // size,),
        in_specs=[
            pl.BlockSpec((rows, inner), lambda i: (0, 0)),
            pl.BlockSpec((size, inner), lambda i: (i, 0)),
        ],
        out_specs=pl.BlockSpec((rows, size), lambda i: (0, i)),
        out_shape=jax.ShapeDtypeStruct((rows, columns), jnp.bfloat16),
        compiler_params=pltpu.CompilerParams(vmem_limit_bytes=40 * 1024 * 1024),
        name="back",
    )(left, right)


def outer_kernel(left_ref, right_ref, out_ref):
    out_ref[...] = inner_rows(left_ref[...], right_ref[...]).astype(jnp.bfloat16)


def outer(left, right):
    rows, wide = left.shape
    columns = right.shape[1]
    size = 2 * BLOCK
    return pl.pallas_call(
        outer_kernel,
        grid=(wide // size,),
        in_specs=[
            pl.BlockSpec((rows, size), lambda i: (0, i)),
            pl.BlockSpec((rows, columns), lambda i: (0, 0)),
        ],
        out_specs=pl.BlockSpec((size, columns), lambda i: (i, 0)),
        out_shape=pltpu.HBM((wide, columns), jnp.bfloat16),
        compiler_params=pltpu.CompilerParams(vmem_limit_bytes=40 * 1024 * 1024),
        name="outer",
    )(left, right)


def times_kernel(left_ref, right_ref, out_ref):
    out_ref[...] = jnp.dot(
        left_ref[...], right_ref[...], preferred_element_type=jnp.float32
    ).astype(jnp.bfloat16)


def times(left, right):
    rows, inner = left.shape
    columns = right.shape[1]
    size = 4 * BLOCK
    return pl.pallas_call(
        times_kernel,
        grid=(columns // size,),
        in_specs=[
            pl.BlockSpec((rows, inner), lambda i: (0, 0)),
            pl.BlockSpec((inner, size), lambda i: (0, i)),
        ],
        out_specs=pl.BlockSpec((rows, size), lambda i: (0, i)),
        out_shape=jax.ShapeDtypeStruct((rows, columns), jnp.bfloat16),
        compiler_params=pltpu.CompilerParams(vmem_limit_bytes=40 * 1024 * 1024),
        name="times",
    )(left, right)


def shards(
    tokens,
    seq_lengths,
    seq_order,
    norm_gain,
    query_weight,
    key_value_weight,
    out_weight,
    mlp_gain,
    gate_weight,
    up_weight,
    down_weight,
    cotangent,
):
    rows = tokens.shape[2]
    width = tokens.shape[3]
    group_rows = rows * RING
    q_cols = HEADS // RING * HD
    f_cols = gate_weight.shape[1] // RING
    own_rows = query_weight.shape[0]
    shard_index = lax.axis_index("shard")
    seq_index = lax.axis_index("seq")
    grp_index = lax.axis_index("grp")
    own_tokens = tokens[0, 0]
    own_cotangent = cotangent[0, 0]

    gains = jnp.pad(jnp.stack([norm_gain, mlp_gain], axis=1), ((0, 0), (0, HD - 2)))

    def pick_q(i):
        own = lax.dynamic_slice_in_dim(query_weight, i * q_cols, q_cols, 1)
        return jnp.concatenate([own, key_value_weight, gains], axis=1)

    def pick_f(i):
        return jnp.concatenate(
            [
                lax.dynamic_slice_in_dim(gate_weight, i * f_cols, f_cols, 1),
                lax.dynamic_slice_in_dim(up_weight, i * f_cols, f_cols, 1),
            ],
            axis=1,
        )

    group_start = shard_index * group_rows
    ring_rows = (seq_index + jnp.arange(RING, dtype=jnp.int32)) % RING * rows
    in_group = (ring_rows[:, None] + jnp.arange(rows, dtype=jnp.int32)[None, :]).reshape(-1)
    query_index = group_start + in_group
    starts = slot_starts(seq_lengths[0], seq_order[0])
    begins = jnp.max(
        jnp.where(query_index[:, None] >= starts[None, :], starts[None, :], 0), axis=1
    )
    cos, sin = rotation(query_index - begins)
    info = jnp.concatenate([jnp.stack([shard_index, seq_index]).astype(jnp.int32), starts])

    def scattered(grad, dim):
        return lax.psum_scatter(grad, "shard", scatter_dimension=dim, tiled=True)

    w_out = lax.all_gather(out_weight, "shard", axis=0, tiled=True)
    got = exchange_parts(pick_q, "seq", seq_index)
    tok_after = send(own_tokens, "seq", -1)
    tok_before = send(own_tokens, "seq", 1)
    *got, tok_after, tok_before, gate_weight, up_weight, down_weight = fence(
        *got, tok_after, tok_before, gate_weight, up_weight, down_weight
    )
    w_down = lax.all_gather(down_weight, "shard", axis=0, tiled=True)
    block = jnp.stack(got)
    block_after = send_x(block, -1)
    block_before = send_x(block, 1)
    half = rows // 2
    tok_far_a = send(tok_after[:half], "seq", -1)
    tok_far_b = send(tok_before[half:], "seq", 1)
    block_after, block_before, tok_far_a, tok_far_b, gate_weight, up_weight, w_out = fence(
        block_after, block_before, tok_far_a, tok_far_b, gate_weight, up_weight, w_out
    )
    block_far_a = send_x(block_after[: RING // 2], -1)
    block_far_b = send_x(block_before[RING // 2 :], 1)
    near = send_core(jnp.stack([block, block_after, block_before]))
    got = exchange_parts(pick_f, "seq", seq_index)
    tokens_bf = jnp.concatenate([own_tokens, tok_after, tok_far_a, tok_far_b, tok_before], axis=0)
    block_far_a, block_far_b, near, tokens_bf = fence(block_far_a, block_far_b, near, tokens_bf)
    far = send_core(jnp.concatenate([block_far_a, block_far_b]))
    pieces = (block, block_after, block_far_a, block_far_b, block_before, near, far)
    normed_one, queries, pair, scale_one, gain_rows, w_attn = project(
        info, tokens_bf, cos, sin, pieces
    )
    *got, own_cotangent, pair = fence(*got, own_cotangent, pair)
    w_ff = lax.all_gather(by_source(got, seq_index), "shard", axis=1, tiled=True)
    w_ff = w_ff.reshape(width, -1)
    kvs = [shifted(pair, "shard", 2), shifted(pair, "shard", 1), pair]
    *kvs, own_cotangent = fence(*kvs, own_cotangent)
    cot_after = send(own_cotangent, "seq", -1)
    cot_before = send(own_cotangent, "seq", 1)
    gain_one, gain_two = gain_rows[0], gain_rows[1]
    attended, lse = attend(info, queries, kvs)
    attended, cot_after, cot_before, w_down = fence(attended, cot_after, cot_before, w_down)
    cot_far_a = send(cot_after[:half], "seq", -1)
    cot_far_b = send(cot_before[half:], "seq", 1)
    all_cotangent = jnp.concatenate(
        [own_cotangent, cot_after, cot_far_a, cot_far_b, cot_before], axis=0
    )

    branch = scatter_ring(row_blocks(matmul(attended, w_out)), "seq")
    middle = own_tokens.astype(jnp.float32) + branch
    scale_two = norm_scale(middle)
    normed_two = (middle * scale_two * gain_two).astype(jnp.bfloat16)
    n_after = send(normed_two, "seq", -1)
    n_before = send(normed_two, "seq", 1)
    normed_two, n_after, n_before = fence(normed_two, n_after, n_before)
    n_far_a = send(n_after[:half], "seq", -1)
    n_far_b = send(n_before[half:], "seq", 1)
    normed_two = jnp.concatenate([normed_two, n_after, n_far_a, n_far_b, n_before], axis=0)
    grad_hidden, normed_two = fence(inner_cols(all_cotangent, w_down), normed_two)
    hidden, grad_ff = feed(normed_two, grad_hidden, w_ff)
    grad_down = outer(hidden, all_cotangent)
    share_down = scattered(grad_down, 0)
    grad_down, grad_ff = fence(grad_down, grad_ff)
    partial_two = back(grad_ff, w_ff)
    part = own_rows // RING

    def first_half(parts):
        return send(parts[2][:half], "seq", 1), send(parts[2][half:], "seq", -1)

    def second_half(parts, got_a, got_b):
        one, last = [parts[i].astype(jnp.float32) for i in (1, 3)]
        one = jnp.concatenate([one[:half] + got_a.astype(jnp.float32), one[half:]], axis=0)
        last = jnp.concatenate([last[:half], last[half:] + got_b.astype(jnp.float32)], axis=0)
        return (
            send(one.astype(jnp.bfloat16), "seq", 1),
            send(last.astype(jnp.bfloat16), "seq", -1),
        )

    def total(*blocks):
        return sum(block.astype(jnp.float32) for block in blocks)

    parts = row_blocks(partial_two)
    two_a, two_b = first_half(parts)
    two_a, two_b, grad_ff = fence(two_a, two_b, grad_ff)
    from_last, from_next = second_half(parts, two_a, two_b)
    grad_wff = outer(normed_two, grad_ff)
    from_last, from_next, grad_wff, hidden = fence(from_last, from_next, grad_wff, hidden)
    share_ff = scattered(grad_wff.reshape(RING, -1, 2 * f_cols), 1)
    grad_normed_two = total(parts[0], from_last, from_next)
    grad_middle = own_cotangent.astype(jnp.float32) + norm_back(
        middle, scale_two, gain_two, grad_normed_two
    )
    own_branch = grad_middle.astype(jnp.bfloat16)

    gb_after = send(own_branch, "seq", -1)
    gb_before = send(own_branch, "seq", 1)
    out_parts = times(hidden, w_down)
    gb_after, gb_before, out_parts, own_branch, share_down = fence(
        gb_after, gb_before, out_parts, own_branch, share_down
    )
    gb_far_a = send(gb_after[:half], "seq", -1)
    gb_far_b = send(gb_before[half:], "seq", 1)
    gb_far_a, gb_far_b, share_down = fence(gb_far_a, gb_far_b, share_down)
    grad_branch = jnp.concatenate([own_branch, gb_after, gb_far_a, gb_far_b, gb_before], axis=0)
    grad_attended = inner_cols(grad_branch, w_out).astype(jnp.bfloat16)

    down_pieces = exchange_parts(
        lambda i: lax.dynamic_index_in_dim(
            share_down.reshape(RING, -1, width), i, 0, keepdims=False
        ),
        "grp",
        grp_index,
    )
    grad_queries, grad_table = attend_back(info, queries, grad_attended, lse, cos, sin, kvs)
    grad_queries, grad_table, *down_pieces = fence(grad_queries, grad_table, *down_pieces)

    returned_two = shifted(grad_table[0].astype(jnp.bfloat16), "shard", -2)
    returned_one = shifted(grad_table[1].astype(jnp.bfloat16), "shard", -1)

    def grp_pieces(share, dim):
        return exchange_parts(
            lambda i: lax.dynamic_index_in_dim(share, i, dim, keepdims=False), "grp", grp_index
        )

    def seq_pieces(summed):
        return exchange_parts(
            lambda i: lax.dynamic_index_in_dim(summed, i, 0, keepdims=False), "seq", seq_index
        )

    def side_by_side(columns):
        return columns.transpose(1, 0, 2).reshape(columns.shape[1], -1)

    returned_one, returned_two, grad_table, *down_pieces = fence(
        returned_one, returned_two, grad_table, *down_pieces
    )
    grad_pair = total(grad_table[2], returned_one, returned_two)
    grad_keys = grad_pair[:, :HD]
    swapped = jnp.concatenate([grad_keys[:, HD // 2 :], grad_keys[:, : HD // 2]], axis=1)
    grad_keys = grad_keys * cos - swapped * sin
    grad_pair = jnp.concatenate([grad_keys, grad_pair[:, HD:]], axis=1).astype(jnp.bfloat16)
    gain_two_terms = (grad_normed_two * middle * scale_two).astype(jnp.bfloat16)
    partial_one, grad_attn = unproject(
        grad_queries, grad_pair, w_attn, normed_one, tokens_bf, scale_one, attended, grad_branch,
        gain_two_terms,
    )
    parts, outs = row_blocks(partial_one), row_blocks(out_parts)
    one_a = send(parts[2], "seq", 1)
    one_b = send(outs[2], "seq", -1)
    n_attn = w_attn.shape[1]
    share_attn = scattered(grad_attn.reshape(RING, -1, grad_attn.shape[1]), 1)
    one_a, one_b, share_ff, *down_pieces = fence(one_a, one_b, share_ff, *down_pieces)
    after = jnp.concatenate([total(parts[1], one_a).astype(jnp.bfloat16), outs[1]], axis=0)
    before = jnp.concatenate([parts[3], total(outs[3], one_b).astype(jnp.bfloat16)], axis=0)
    from_last = send(after, "seq", 1)
    from_next = send(before, "seq", -1)
    ff_pieces = grp_pieces(share_ff.reshape(RING, RING, part, -1), 1)
    from_last, from_next, *ff_pieces = fence(from_last, from_next, *ff_pieces)
    ff_pieces = seq_pieces(total(*ff_pieces).astype(jnp.bfloat16))
    down_own = total(*down_pieces).astype(jnp.bfloat16)
    down_got = [send(down_own, "grp", -k) for k in range(1, RING)]
    down_got, ff_pieces = fence(down_got, ff_pieces)
    share_down = ordered([down_own] + down_got, grp_index).reshape(-1, width)
    share_down = share_down.astype(jnp.float32)
    ff_columns = by_source(ff_pieces, seq_index)
    ff_rows = jnp.concatenate(
        [side_by_side(ff_columns[:, :, :f_cols]), side_by_side(ff_columns[:, :, f_cols:])], axis=1
    )
    ff_after = send(ff_rows, "grp", -1)
    ff_before = send(ff_rows, "grp", 1)
    grad_normed_one = total(parts[0], from_last[:rows], from_next[:rows])
    result = middle + total(outs[0], from_last[rows:], from_next[rows:])
    layer_output = result.astype(jnp.bfloat16)[None, None]
    own_inputs = own_tokens.astype(jnp.float32)
    input_grad = grad_middle + norm_back(
        own_inputs, norm_scale(own_inputs), gain_one, grad_normed_one
    )
    ff_after, ff_before, input_grad, layer_output, share_attn = fence(
        ff_after, ff_before, input_grad, layer_output, share_attn
    )
    ff_far_a = send(ff_after[: part // 2], "grp", -1)
    ff_far_b = send(ff_before[part // 2 :], "grp", 1)
    pieces = grp_pieces(share_attn.reshape(RING, RING, part, -1), 1)
    ff_far_a, ff_far_b, ff_rows, *pieces = fence(ff_far_a, ff_far_b, ff_rows, *pieces)
    ff_far = jnp.concatenate([ff_far_a, ff_far_b], axis=0)
    ff_rows = ordered([ff_rows, ff_after, ff_far, ff_before], grp_index)
    ff_rows = ff_rows.reshape(own_rows, -1).astype(jnp.float32)
    share_gate = ff_rows[:, : RING * f_cols]
    share_upper = ff_rows[:, RING * f_cols :]
    summed = total(*pieces).astype(jnp.bfloat16)
    out_own = side_by_side(summed[:, :, n_attn:])
    columns = by_source(seq_pieces(summed[:, :, :n_attn]), seq_index)
    summed = total(*[columns[i, :, q_cols:] for i in range(RING)]).astype(jnp.bfloat16)
    attn_rows = jnp.concatenate(
        [side_by_side(columns[:, :, :q_cols]), out_own, summed], axis=1
    )
    attn_got = [send(attn_rows, "grp", -k) for k in range(1, RING)]
    attn_rows = ordered([attn_rows] + attn_got, grp_index).reshape(own_rows, -1)
    attn_rows = attn_rows.astype(jnp.float32)
    share_query = attn_rows[:, :width]
    share_out = attn_rows[:, width : 2 * width]
    share_pair = attn_rows[:, 2 * width : 2 * width + 2 * HD]
    share_gain_one = attn_rows[:, 2 * width + 2 * HD]
    share_gain_two = attn_rows[:, 2 * width + 2 * HD + 1]
    return (
        layer_output,
        input_grad[None, None],
        share_gain_one,
        share_query,
        share_pair,
        share_out,
        share_gain_two,
        share_gate,
        share_upper,
        share_down,
    )


def solution(mesh):
    by_row = P(("seq", "shard"), None)
    by_entry = P(("seq", "shard"))
    by_token = P("grp", "shard", "seq", None)
    return jax.shard_map(
        shards,
        mesh=mesh,
        in_specs=(
            by_token,
            P("grp", None),
            P("grp", None),
            by_entry,
            by_row,
            by_row,
            by_row,
            by_entry,
            by_row,
            by_row,
            by_row,
            by_token,
        ),
        out_specs=(
            by_token,
            by_token,
            by_entry,
            by_row,
            by_row,
            by_row,
            by_entry,
            by_row,
            by_row,
            by_row,
        ),
        check_vma=False,
    )
```

```python
import functools

import jax
import jax.numpy as jnp
from jax import lax
from jax.experimental import pallas as pl
from jax.experimental.pallas import tpu as pltpu
from jax.sharding import PartitionSpec as P

HEADS = 16
HD = 128
WINDOW = 1024
RING = 4
BLOCK = 128
CHUNK = 32
FBLOCK = 512

epsilon = 1e-06
big_negative = -1e30


def send(value, axis, steps):
    count = lax.axis_size(axis)
    return lax.ppermute(value, axis, [(i, (i + steps) % count) for i in range(count)])


def send_x(value, steps):
    return lax.ppermute(
        value,
        "shard",
        [(x * 2 + c, (x + steps) % RING * 2 + c) for x in range(RING) for c in range(2)],
    )


def send_core(value):
    return lax.ppermute(
        value, "shard", [(x * 2 + c, x * 2 + 1 - c) for x in range(RING) for c in range(2)]
    )


def fence(*values):
    return lax.optimization_barrier(values)


def shifted(value, axis, steps):
    count = lax.axis_size(axis)
    initial, last = (max(0, -steps), min(count, count - steps))
    return lax.ppermute(value, axis, [(i, i + steps) for i in range(initial, last)])


def scatter_ring(parts, axis):
    far = parts[2]
    own, nxt, prv = [parts[i].astype(jnp.float32) for i in (0, 1, 3)]
    half = own.shape[0] // 2
    got_a = send(far[:half].astype(jnp.bfloat16), axis, 1).astype(jnp.float32)
    got_b = send(far[half:].astype(jnp.bfloat16), axis, -1).astype(jnp.float32)
    nxt = jnp.concatenate([nxt[:half] + got_a, nxt[half:]], axis=0)
    prv = jnp.concatenate([prv[:half], prv[half:] + got_b], axis=0)
    from_prv = send(nxt.astype(jnp.bfloat16), axis, 1).astype(jnp.float32)
    from_nxt = send(prv.astype(jnp.bfloat16), axis, -1).astype(jnp.float32)
    return own + from_prv + from_nxt


def ordered(parts, index):
    return jnp.stack(
        [
            lax.select_n(index, *[parts[(place - m) % RING] for m in range(RING)])
            for place in range(RING)
        ],
        axis=0,
    )


def exchange_parts(pick, axis, index):
    got = [pick((index + k) % RING) for k in range(RING)]
    return [got[0]] + [send(got[k], axis, k) for k in range(1, RING)]


def by_source(got, index):
    return ordered([got[0], got[3], got[2], got[1]], index)


def exchange(pick, axis, index):
    return by_source(exchange_parts(pick, axis, index), index)


def row_blocks(total):
    rows = total.shape[0] // RING
    return [total[i * rows : (i + 1) * rows] for i in range(RING)]


def norm_scale(values):
    return lax.rsqrt(jnp.mean(values * values, axis=-1, keepdims=True) + epsilon)


def norm_back(values, scale, gain, grad):
    scaled = grad * gain
    dot = jnp.mean(scaled * values, axis=-1, keepdims=True)
    return scaled * scale - values * (scale * scale * scale * dot)


def slot_starts(lengths, packing):
    slots = jnp.arange(lengths.shape[0], dtype=jnp.int32)
    picked = (packing[:, None] == slots[None, :]).astype(jnp.int32)
    packed = jnp.sum(picked * lengths[None, :], axis=1, dtype=jnp.int32)
    return jnp.cumsum(packed, dtype=jnp.int32) - packed


def rotation(place):
    half_width = HD // 2
    frequency = 10000.0 ** (-jnp.arange(half_width, dtype=jnp.float32) / half_width)
    angle = place.astype(jnp.float32)[:, None] * frequency
    cosine, sine = jnp.cos(angle), jnp.sin(angle)
    return jnp.concatenate([cosine, cosine], axis=1), jnp.concatenate([-sine, sine], axis=1)


def matmul(left, right):
    return jnp.dot(left, right, preferred_element_type=jnp.float32)


def inner_rows(left, right):
    return lax.dot_general(
        left, right, (((0,), (0,)), ((), ())), preferred_element_type=jnp.float32
    )


def inner_cols(left, right):
    return lax.dot_general(
        left, right, (((1,), (1,)), ((), ())), preferred_element_type=jnp.float32
    )


def tile_mask(info, tile, first_row, rows, reach, group):
    shard, seq = info[0], info[1]
    base = shard * group
    row = lax.broadcasted_iota(jnp.int32, (rows, 1), 0) + first_row
    query = base + (seq + tile) % RING * BLOCK + row
    begin = jnp.zeros_like(query)
    for slot in range(info.shape[0] - 2):
        start = info[2 + slot]
        begin = jnp.where(query >= start, jnp.maximum(begin, start), begin)
    lowest = jnp.maximum(begin, query - (WINDOW - 1))
    lane = lax.broadcasted_iota(jnp.int32, (1, reach), 1)
    block = lane // group
    in_block = lane - block * group
    key = base + (block - (reach // group - 1)) * group
    key = key + (seq + in_block // BLOCK) % RING * BLOCK + in_block % BLOCK
    return (key <= query) & (key >= lowest)


def attend_kernel(info, q_ref, *refs, heads, group):
    kv_refs, (out_ref, lse_ref, scores_ref, soft_ref) = refs[:-4], refs[-4:]
    reach = group * len(kv_refs)
    tile = pl.program_id(0)
    q = jnp.concatenate([q_ref[:, h * HD : (h + 1) * HD] for h in range(heads)], axis=0)
    for b, kv in enumerate(kv_refs):
        scores_ref[:, b * group : (b + 1) * group] = inner_cols(q, kv[:, :HD])
    for part in range(BLOCK // CHUNK):
        mask = tile_mask(info, tile, part * CHUNK, CHUNK, reach, group)
        for h in range(heads):
            at = pl.ds(h * BLOCK + part * CHUNK, CHUNK)
            scores = jnp.where(mask, scores_ref[at, :] * (HD**-0.5), big_negative)
            top = jnp.max(scores, axis=1, keepdims=True)
            expo = jnp.exp(scores - top)
            total = jnp.sum(expo, axis=1, keepdims=True)
            soft_ref[at, :] = (expo * (1.0 / total)).astype(jnp.bfloat16)
            lse_ref[0, at, :] = jnp.broadcast_to(top + jnp.log(total), (CHUNK, HD))
    acc = None
    for b, kv in enumerate(kv_refs):
        term = jnp.dot(soft_ref[:, b * group : (b + 1) * group], kv[:, HD:], preferred_element_type=jnp.float32)
        acc = term if acc is None else acc + term
    for h in range(heads):
        out_ref[:, h * HD : (h + 1) * HD] = acc[h * BLOCK : (h + 1) * BLOCK].astype(jnp.bfloat16)


def attend(info, queries, kvs):
    group, width = queries.shape
    heads = width // HD
    reach = group * len(kvs)
    whole = pl.BlockSpec((group, 2 * HD), lambda i: (0, 0))
    rows = pl.BlockSpec((BLOCK, width), lambda i: (i, 0))
    return pl.pallas_call(
        functools.partial(attend_kernel, heads=heads, group=group),
        grid=(group // BLOCK,),
        in_specs=[pl.BlockSpec(memory_space=pltpu.SMEM), rows] + [whole] * len(kvs),
        out_specs=[rows, pl.BlockSpec((1, heads * BLOCK, HD), lambda i: (i, 0, 0))],
        out_shape=[
            jax.ShapeDtypeStruct((group, width), jnp.bfloat16),
            jax.ShapeDtypeStruct((group // BLOCK, heads * BLOCK, HD), jnp.float32),
        ],
        scratch_shapes=[
            pltpu.VMEM((heads * BLOCK, reach), jnp.float32),
            pltpu.VMEM((heads * BLOCK, reach), jnp.bfloat16),
        ],
        compiler_params=pltpu.CompilerParams(vmem_limit_bytes=40 * 1024 * 1024),
        name="attend",
    )(info, queries, *kvs)


def attend_back_kernel(info, q_ref, do_ref, lse_ref, cos_ref, sin_ref, *refs, heads, group):
    count = len(refs) - 6
    kv_refs, (dq_ref, dkv_ref, scores_ref, dsoft_ref, soft_ref, dscores_ref) = refs[:count], refs[count:]
    reach = group * count
    tile = pl.program_id(0)

    @pl.when(tile == 0)
    def _():
        dkv_ref[...] = jnp.zeros_like(dkv_ref)

    q = jnp.concatenate([q_ref[:, h * HD : (h + 1) * HD] for h in range(heads)], axis=0)
    do = jnp.concatenate([do_ref[:, h * HD : (h + 1) * HD] for h in range(heads)], axis=0)
    for b, kv in enumerate(kv_refs):
        at = slice(b * group, (b + 1) * group)
        scores_ref[:, at] = inner_cols(q, kv[:, :HD])
        dsoft_ref[:, at] = inner_cols(do, kv[:, HD:])
    for part in range(BLOCK // CHUNK):
        mask = tile_mask(info, tile, part * CHUNK, CHUNK, reach, group)
        for h in range(heads):
            at = pl.ds(h * BLOCK + part * CHUNK, CHUNK)
            lse = lse_ref[0, at, 0:1]
            scores = jnp.where(mask, scores_ref[at, :] * (HD**-0.5), big_negative)
            soft = jnp.exp(scores - lse)
            dsoft = dsoft_ref[at, :]
            delta = jnp.sum(soft * dsoft, axis=1, keepdims=True)
            soft_ref[at, :] = soft.astype(jnp.bfloat16)
            dscores_ref[at, :] = (soft * (dsoft - delta)).astype(jnp.bfloat16)
    dq = None
    for b, kv in enumerate(kv_refs):
        at = slice(b * group, (b + 1) * group)
        term = jnp.dot(dscores_ref[:, at], kv[:, :HD], preferred_element_type=jnp.float32)
        dq = term if dq is None else dq + term
        dkv_ref[b, :, :HD] += inner_rows(dscores_ref[:, at], q) * (HD**-0.5)
        dkv_ref[b, :, HD:] += inner_rows(soft_ref[:, at], do)
    cos, sin = cos_ref[...], sin_ref[...]
    for h in range(heads):
        one = dq[h * BLOCK : (h + 1) * BLOCK] * (HD**-0.5)
        one = one * cos - pltpu.roll(one, HD // 2, 1) * sin
        dq_ref[:, h * HD : (h + 1) * HD] = one.astype(jnp.bfloat16)


def attend_back(info, queries, grads, lse, cos, sin, kvs):
    group, width = queries.shape
    heads = width // HD
    reach = group * len(kvs)
    whole = pl.BlockSpec((group, 2 * HD), lambda i: (0, 0))
    rows = pl.BlockSpec((BLOCK, width), lambda i: (i, 0))
    table = pl.BlockSpec((BLOCK, HD), lambda i: (i, 0))
    return pl.pallas_call(
        functools.partial(attend_back_kernel, heads=heads, group=group),
        grid=(group // BLOCK,),
        in_specs=[
            pl.BlockSpec(memory_space=pltpu.SMEM),
            rows,
            rows,
            pl.BlockSpec((1, heads * BLOCK, HD), lambda i: (i, 0, 0)),
            table,
            table,
        ]
        + [whole] * len(kvs),
        out_specs=[rows, pl.BlockSpec((len(kvs), group, 2 * HD), lambda i: (0, 0, 0))],
        out_shape=[
            jax.ShapeDtypeStruct((group, width), jnp.bfloat16),
            jax.ShapeDtypeStruct((len(kvs), group, 2 * HD), jnp.float32),
        ],
        scratch_shapes=[
            pltpu.VMEM((heads * BLOCK, reach), jnp.float32),
            pltpu.VMEM((heads * BLOCK, reach), jnp.float32),
            pltpu.VMEM((heads * BLOCK, reach), jnp.bfloat16),
            pltpu.VMEM((heads * BLOCK, reach), jnp.bfloat16),
        ],
        compiler_params=pltpu.CompilerParams(vmem_limit_bytes=40 * 1024 * 1024),
        name="attend_back",
    )(info, queries, grads, lse, cos, sin, *kvs)


def project_kernel(
    info, tok_ref, cos_ref, sin_ref, own, after, far_a, far_b, before, near, far,
    n_ref, q_ref, kv_ref, scale_ref, gains_ref, w_ref, sems, *, heads, block
):
    q_cols = heads * HD

    @pl.when(pl.program_id(0) == 0)
    def _():
        x, core, seq = info[0] // 2, info[0] % 2, info[1]
        copies = []

        def fetch(piece, k, other, first):
            place = (x + k) % RING * 2 + (1 - core if other else core)
            for i in range(piece.shape[0]):
                source = (seq - first - i + RING) % RING
                at = pl.multiple_of(source * 8 * block + place * block, block)
                copies.append(
                    pltpu.make_async_copy(
                        piece.at[i], w_ref.at[pl.ds(at, block), :], sems.at[len(copies)]
                    )
                )

        half = RING // 2
        fetch(own, 0, False, 0)
        fetch(after, 1, False, 0)
        fetch(far_a, 2, False, 0)
        fetch(far_b, 2, False, half)
        fetch(before, 3, False, 0)
        fetch(near.at[0], 0, True, 0)
        fetch(near.at[1], 1, True, 0)
        fetch(far, 2, True, 0)
        fetch(near.at[2], 3, True, 0)
        for copy in copies:
            copy.start()
        for copy in copies:
            copy.wait()
        pick = lax.broadcasted_iota(jnp.int32, (8, HD), 0) == lax.broadcasted_iota(
            jnp.int32, (8, HD), 1
        )
        gains_ref[...] = inner_cols(pick.astype(jnp.bfloat16), w_ref[:, q_cols + 2 * HD :])

    x = tok_ref[...].astype(jnp.float32)
    scale = lax.rsqrt(jnp.mean(x * x, axis=1, keepdims=True) + epsilon)
    normed = (x * scale * gains_ref[0:1, :]).astype(jnp.bfloat16)
    n_ref[...] = normed
    scale_ref[...] = jnp.broadcast_to(scale, scale_ref.shape)
    qkv = jnp.dot(normed, w_ref[:, : q_cols + 2 * HD], preferred_element_type=jnp.float32)
    cos, sin = cos_ref[...], sin_ref[...]
    for h in range(heads + 1):
        one = qkv[:, h * HD : (h + 1) * HD]
        one = (one * cos + pltpu.roll(one, HD // 2, 1) * sin).astype(jnp.bfloat16)
        if h < heads:
            q_ref[:, h * HD : (h + 1) * HD] = one
        else:
            kv_ref[:, :HD] = one
    kv_ref[:, HD:] = qkv[:, (heads + 1) * HD :].astype(jnp.bfloat16)


def project(info, tokens, cos, sin, pieces):
    group, width = tokens.shape
    block, columns = pieces[0].shape[1:]
    heads = columns // HD - 3
    rows = lambda n: pl.BlockSpec((BLOCK, n), lambda i: (i, 0))
    whole = lambda shape: pl.BlockSpec(shape, lambda i: (0, 0))
    return pl.pallas_call(
        functools.partial(project_kernel, heads=heads, block=block),
        grid=(group // BLOCK,),
        in_specs=[pl.BlockSpec(memory_space=pltpu.SMEM), rows(width), rows(HD), rows(HD)]
        + [pl.BlockSpec(memory_space=pl.ANY)] * len(pieces),
        out_specs=[
            rows(width),
            rows(heads * HD),
            rows(2 * HD),
            rows(HD),
            whole((8, width)),
            whole((width, columns)),
        ],
        out_shape=[
            jax.ShapeDtypeStruct((group, width), jnp.bfloat16),
            jax.ShapeDtypeStruct((group, heads * HD), jnp.bfloat16),
            jax.ShapeDtypeStruct((group, 2 * HD), jnp.bfloat16),
            jax.ShapeDtypeStruct((group, HD), jnp.float32),
            jax.ShapeDtypeStruct((8, width), jnp.float32),
            jax.ShapeDtypeStruct((width, columns), jnp.bfloat16),
        ],
        scratch_shapes=[pltpu.SemaphoreType.DMA((8 * RING,))],
        compiler_params=pltpu.CompilerParams(vmem_limit_bytes=40 * 1024 * 1024),
        name="project",
    )(info, tokens, cos, sin, *pieces)


def unproject_kernel(
    dq_ref, dkv_ref, w_ref, n_ref, tok_ref, scale_ref, att_ref, branch_ref, two_ref,
    part_ref, grad_ref
):
    q_cols = dq_ref.shape[1]
    n_attn = w_ref.shape[1]
    grads = jnp.concatenate([dq_ref[...], dkv_ref[...]], axis=1)
    part = inner_cols(grads, w_ref[:, : q_cols + 2 * HD])
    part_ref[...] = part.astype(jnp.bfloat16)
    terms = (part * tok_ref[...].astype(jnp.float32) * scale_ref[:, 0:1]).astype(jnp.bfloat16)
    column = lax.broadcasted_iota(jnp.int32, (part.shape[0], HD), 1)
    first = (column == 0).astype(jnp.bfloat16)
    second = (column == 1).astype(jnp.bfloat16)[: two_ref.shape[0]]
    grad_ref[:, : q_cols + 2 * HD] = inner_rows(n_ref[...], grads).astype(jnp.bfloat16)
    gains = inner_rows(terms, first) + inner_rows(two_ref[...], second)
    grad_ref[:, q_cols + 2 * HD : n_attn] = gains.astype(jnp.bfloat16)
    grad_ref[:, n_attn:] = inner_rows(att_ref[...], branch_ref[...]).astype(jnp.bfloat16)


def unproject(
    grad_queries, grad_pair, weights, normed, tokens, scale, attended, grad_branch, two
):
    group, width = tokens.shape
    size = 4 * BLOCK
    columns = weights.shape[1]
    whole = lambda n: pl.BlockSpec((group, n), lambda i: (0, 0))
    across = pl.BlockSpec((group, size), lambda i: (0, i))
    down = pl.BlockSpec((size, columns), lambda i: (i, 0))
    return pl.pallas_call(
        unproject_kernel,
        grid=(width // size,),
        in_specs=[
            whole(grad_queries.shape[1]),
            whole(grad_pair.shape[1]),
            down,
            across,
            across,
            whole(HD),
            whole(attended.shape[1]),
            across,
            pl.BlockSpec((two.shape[0], size), lambda i: (0, i)),
        ],
        out_specs=[across, pl.BlockSpec((size, columns + size), lambda i: (i, 0))],
        out_shape=[
            jax.ShapeDtypeStruct((group, width), jnp.bfloat16),
            jax.ShapeDtypeStruct((width, columns + size), jnp.bfloat16),
        ],
        compiler_params=pltpu.CompilerParams(vmem_limit_bytes=40 * 1024 * 1024),
        name="unproject",
    )(grad_queries, grad_pair, weights, normed, tokens, scale, attended, grad_branch, two)


def feed_kernel(n_ref, gh_ref, gate_ref, up_ref, hidden_ref, grad_ref):
    step = pl.program_id(0)
    size = gate_ref.shape[1]
    inner = grad_ref.shape[1] // 2
    gate = jnp.dot(n_ref[...], gate_ref[...], preferred_element_type=jnp.float32)
    upper = jnp.dot(n_ref[...], up_ref[...], preferred_element_type=jnp.float32)
    grad_hidden = gh_ref[...]
    root, cube = 0.7978845608028654, 0.044715
    square = gate * gate
    bend = jnp.tanh(root * gate * (1.0 + cube * square))
    half = 0.5 * (1.0 + bend)
    act = gate * half
    slope = half + 0.5 * gate * (1.0 - bend * bend) * (root * (1.0 + 3.0 * cube * square))
    hidden_ref[...] = (act * upper).astype(jnp.bfloat16)
    grad_gate = (grad_hidden * upper * slope).astype(jnp.bfloat16)
    grad_upper = (grad_hidden * act).astype(jnp.bfloat16)
    grad_ref[:, pl.ds(pl.multiple_of(step * size, size), size)] = grad_gate
    grad_ref[:, pl.ds(pl.multiple_of(inner + step * size, size), size)] = grad_upper


def feed(normed, grad_hidden, weights):
    group, width = normed.shape
    inner = grad_hidden.shape[1]
    steps = inner // FBLOCK
    whole = lambda n: pl.BlockSpec((group, n), lambda i: (0, 0))
    columns = pl.BlockSpec((group, FBLOCK), lambda i: (0, i))
    return pl.pallas_call(
        feed_kernel,
        grid=(steps,),
        in_specs=[
            whole(width),
            columns,
            pl.BlockSpec((width, FBLOCK), lambda i: (0, i)),
            pl.BlockSpec((width, FBLOCK), lambda i: (0, steps + i)),
        ],
        out_specs=[columns, whole(2 * inner)],
        out_shape=[
            jax.ShapeDtypeStruct((group, inner), jnp.bfloat16),
            jax.ShapeDtypeStruct((group, 2 * inner), jnp.bfloat16),
        ],
        compiler_params=pltpu.CompilerParams(vmem_limit_bytes=48 * 1024 * 1024),
        name="feed",
    )(normed, grad_hidden, weights, weights)


def back_kernel(left_ref, right_ref, out_ref):
    out_ref[...] = inner_cols(left_ref[...], right_ref[...]).astype(jnp.bfloat16)


def back(left, right):
    rows, inner = left.shape
    columns = right.shape[0]
    size = 4 * BLOCK
    return pl.pallas_call(
        back_kernel,
        grid=(columns // size,),
        in_specs=[
            pl.BlockSpec((rows, inner), lambda i: (0, 0)),
            pl.BlockSpec((size, inner), lambda i: (i, 0)),
        ],
        out_specs=pl.BlockSpec((rows, size), lambda i: (0, i)),
        out_shape=jax.ShapeDtypeStruct((rows, columns), jnp.bfloat16),
        compiler_params=pltpu.CompilerParams(vmem_limit_bytes=40 * 1024 * 1024),
        name="back",
    )(left, right)


def outer_kernel(left_ref, right_ref, out_ref):
    out_ref[...] = inner_rows(left_ref[...], right_ref[...]).astype(jnp.bfloat16)


def outer(left, right):
    rows, wide = left.shape
    columns = right.shape[1]
    size = 2 * BLOCK
    return pl.pallas_call(
        outer_kernel,
        grid=(wide // size,),
        in_specs=[
            pl.BlockSpec((rows, size), lambda i: (0, i)),
            pl.BlockSpec((rows, columns), lambda i: (0, 0)),
        ],
        out_specs=pl.BlockSpec((size, columns), lambda i: (i, 0)),
        out_shape=pltpu.HBM((wide, columns), jnp.bfloat16),
        compiler_params=pltpu.CompilerParams(vmem_limit_bytes=40 * 1024 * 1024),
        name="outer",
    )(left, right)


def times_kernel(left_ref, right_ref, out_ref):
    out_ref[...] = jnp.dot(
        left_ref[...], right_ref[...], preferred_element_type=jnp.float32
    ).astype(jnp.bfloat16)


def times(left, right):
    rows, inner = left.shape
    columns = right.shape[1]
    size = 4 * BLOCK
    return pl.pallas_call(
        times_kernel,
        grid=(columns // size,),
        in_specs=[
            pl.BlockSpec((rows, inner), lambda i: (0, 0)),
            pl.BlockSpec((inner, size), lambda i: (0, i)),
        ],
        out_specs=pl.BlockSpec((rows, size), lambda i: (0, i)),
        out_shape=jax.ShapeDtypeStruct((rows, columns), jnp.bfloat16),
        compiler_params=pltpu.CompilerParams(vmem_limit_bytes=40 * 1024 * 1024),
        name="times",
    )(left, right)


def shards(
    tokens,
    seq_lengths,
    seq_order,
    norm_gain,
    query_weight,
    key_value_weight,
    out_weight,
    mlp_gain,
    gate_weight,
    up_weight,
    down_weight,
    cotangent,
):
    rows = tokens.shape[2]
    width = tokens.shape[3]
    group_rows = rows * RING
    q_cols = HEADS // RING * HD
    f_cols = gate_weight.shape[1] // RING
    own_rows = query_weight.shape[0]
    shard_index = lax.axis_index("shard")
    seq_index = lax.axis_index("seq")
    grp_index = lax.axis_index("grp")
    own_tokens = tokens[0, 0]
    own_cotangent = cotangent[0, 0]

    gains = jnp.pad(jnp.stack([norm_gain, mlp_gain], axis=1), ((0, 0), (0, HD - 2)))

    def pick_q(i):
        own = lax.dynamic_slice_in_dim(query_weight, i * q_cols, q_cols, 1)
        return jnp.concatenate([own, key_value_weight, gains], axis=1)

    def pick_f(i):
        return jnp.concatenate(
            [
                lax.dynamic_slice_in_dim(gate_weight, i * f_cols, f_cols, 1),
                lax.dynamic_slice_in_dim(up_weight, i * f_cols, f_cols, 1),
            ],
            axis=1,
        )

    group_start = shard_index * group_rows
    ring_rows = (seq_index + jnp.arange(RING, dtype=jnp.int32)) % RING * rows
    in_group = (ring_rows[:, None] + jnp.arange(rows, dtype=jnp.int32)[None, :]).reshape(-1)
    query_index = group_start + in_group
    starts = slot_starts(seq_lengths[0], seq_order[0])
    begins = jnp.max(
        jnp.where(query_index[:, None] >= starts[None, :], starts[None, :], 0), axis=1
    )
    cos, sin = rotation(query_index - begins)
    info = jnp.concatenate([jnp.stack([shard_index, seq_index]).astype(jnp.int32), starts])

    def scattered(grad, dim):
        return lax.psum_scatter(grad, "shard", scatter_dimension=dim, tiled=True)

    w_out = lax.all_gather(out_weight, "shard", axis=0, tiled=True)
    got = exchange_parts(pick_q, "seq", seq_index)
    tok_after = send(own_tokens, "seq", -1)
    tok_before = send(own_tokens, "seq", 1)
    *got, tok_after, tok_before, gate_weight, up_weight, down_weight = fence(
        *got, tok_after, tok_before, gate_weight, up_weight, down_weight
    )
    w_down = lax.all_gather(down_weight, "shard", axis=0, tiled=True)
    block = jnp.stack(got)
    block_after = send_x(block, -1)
    block_before = send_x(block, 1)
    half = rows // 2
    tok_far_a = send(tok_after[:half], "seq", -1)
    tok_far_b = send(tok_before[half:], "seq", 1)
    block_after, block_before, tok_far_a, tok_far_b, gate_weight, up_weight, w_out = fence(
        block_after, block_before, tok_far_a, tok_far_b, gate_weight, up_weight, w_out
    )
    block_far_a = send_x(block_after[: RING // 2], -1)
    block_far_b = send_x(block_before[RING // 2 :], 1)
    near = send_core(jnp.stack([block, block_after, block_before]))
    got = exchange_parts(pick_f, "seq", seq_index)
    tokens_bf = jnp.concatenate([own_tokens, tok_after, tok_far_a, tok_far_b, tok_before], axis=0)
    block_far_a, block_far_b, near, tokens_bf = fence(block_far_a, block_far_b, near, tokens_bf)
    far = send_core(jnp.concatenate([block_far_a, block_far_b]))
    pieces = (block, block_after, block_far_a, block_far_b, block_before, near, far)
    normed_one, queries, pair, scale_one, gain_rows, w_attn = project(
        info, tokens_bf, cos, sin, pieces
    )
    *got, own_cotangent, pair = fence(*got, own_cotangent, pair)
    w_ff = lax.all_gather(by_source(got, seq_index), "shard", axis=1, tiled=True)
    w_ff = w_ff.reshape(width, -1)
    kvs = [shifted(pair, "shard", 2), shifted(pair, "shard", 1), pair]
    *kvs, own_cotangent = fence(*kvs, own_cotangent)
    cot_after = send(own_cotangent, "seq", -1)
    cot_before = send(own_cotangent, "seq", 1)
    gain_one, gain_two = gain_rows[0], gain_rows[1]
    attended, lse = attend(info, queries, kvs)
    attended, cot_after, cot_before, w_down = fence(attended, cot_after, cot_before, w_down)
    cot_far_a = send(cot_after[:half], "seq", -1)
    cot_far_b = send(cot_before[half:], "seq", 1)
    all_cotangent = jnp.concatenate(
        [own_cotangent, cot_after, cot_far_a, cot_far_b, cot_before], axis=0
    )

    branch = scatter_ring(row_blocks(matmul(attended, w_out)), "seq")
    middle = own_tokens.astype(jnp.float32) + branch
    scale_two = norm_scale(middle)
    normed_two = (middle * scale_two * gain_two).astype(jnp.bfloat16)
    n_after = send(normed_two, "seq", -1)
    n_before = send(normed_two, "seq", 1)
    normed_two, n_after, n_before = fence(normed_two, n_after, n_before)
    n_far_a = send(n_after[:half], "seq", -1)
    n_far_b = send(n_before[half:], "seq", 1)
    normed_two = jnp.concatenate([normed_two, n_after, n_far_a, n_far_b, n_before], axis=0)
    grad_hidden, normed_two = fence(inner_cols(all_cotangent, w_down), normed_two)
    hidden, grad_ff = feed(normed_two, grad_hidden, w_ff)
    grad_down = outer(hidden, all_cotangent)
    share_down = scattered(grad_down, 0)
    grad_down, grad_ff = fence(grad_down, grad_ff)
    partial_two = back(grad_ff, w_ff)
    part = own_rows // RING

    def first_half(parts):
        return send(parts[2][:half], "seq", 1), send(parts[2][half:], "seq", -1)

    def second_half(parts, got_a, got_b):
        one, last = [parts[i].astype(jnp.float32) for i in (1, 3)]
        one = jnp.concatenate([one[:half] + got_a.astype(jnp.float32), one[half:]], axis=0)
        last = jnp.concatenate([last[:half], last[half:] + got_b.astype(jnp.float32)], axis=0)
        return (
            send(one.astype(jnp.bfloat16), "seq", 1),
            send(last.astype(jnp.bfloat16), "seq", -1),
        )

    def total(*blocks):
        return sum(block.astype(jnp.float32) for block in blocks)

    parts = row_blocks(partial_two)
    two_a, two_b = first_half(parts)
    two_a, two_b, grad_ff = fence(two_a, two_b, grad_ff)
    from_last, from_next = second_half(parts, two_a, two_b)
    grad_wff = outer(normed_two, grad_ff)
    from_last, from_next, grad_wff, hidden = fence(from_last, from_next, grad_wff, hidden)
    share_ff = scattered(grad_wff.reshape(RING, -1, 2 * f_cols), 1)
    grad_normed_two = total(parts[0], from_last, from_next)
    grad_middle = own_cotangent.astype(jnp.float32) + norm_back(
        middle, scale_two, gain_two, grad_normed_two
    )
    own_branch = grad_middle.astype(jnp.bfloat16)

    gb_after = send(own_branch, "seq", -1)
    gb_before = send(own_branch, "seq", 1)
    out_parts = times(hidden, w_down)
    gb_after, gb_before, out_parts, own_branch, share_down = fence(
        gb_after, gb_before, out_parts, own_branch, share_down
    )
    gb_far_a = send(gb_after[:half], "seq", -1)
    gb_far_b = send(gb_before[half:], "seq", 1)
    gb_far_a, gb_far_b, share_down = fence(gb_far_a, gb_far_b, share_down)
    grad_branch = jnp.concatenate([own_branch, gb_after, gb_far_a, gb_far_b, gb_before], axis=0)
    grad_attended = inner_cols(grad_branch, w_out).astype(jnp.bfloat16)

    down_pieces = exchange_parts(
        lambda i: lax.dynamic_index_in_dim(
            share_down.reshape(RING, -1, width), i, 0, keepdims=False
        ),
        "grp",
        grp_index,
    )
    grad_queries, grad_table = attend_back(info, queries, grad_attended, lse, cos, sin, kvs)
    grad_queries, grad_table, *down_pieces = fence(grad_queries, grad_table, *down_pieces)

    returned_two = shifted(grad_table[0].astype(jnp.bfloat16), "shard", -2)
    returned_one = shifted(grad_table[1].astype(jnp.bfloat16), "shard", -1)

    def grp_pieces(share, dim):
        return exchange_parts(
            lambda i: lax.dynamic_index_in_dim(share, i, dim, keepdims=False), "grp", grp_index
        )

    def seq_pieces(summed):
        return exchange_parts(
            lambda i: lax.dynamic_index_in_dim(summed, i, 0, keepdims=False), "seq", seq_index
        )

    def side_by_side(columns):
        return columns.transpose(1, 0, 2).reshape(columns.shape[1], -1)

    returned_one, returned_two, grad_table, *down_pieces = fence(
        returned_one, returned_two, grad_table, *down_pieces
    )
    grad_pair = total(grad_table[2], returned_one, returned_two)
    grad_keys = grad_pair[:, :HD]
    swapped = jnp.concatenate([grad_keys[:, HD // 2 :], grad_keys[:, : HD // 2]], axis=1)
    grad_keys = grad_keys * cos - swapped * sin
    grad_pair = jnp.concatenate([grad_keys, grad_pair[:, HD:]], axis=1).astype(jnp.bfloat16)
    gain_two_terms = (grad_normed_two * middle * scale_two).astype(jnp.bfloat16)
    partial_one, grad_attn = unproject(
        grad_queries, grad_pair, w_attn, normed_one, tokens_bf, scale_one, attended, grad_branch,
        gain_two_terms,
    )
    parts, outs = row_blocks(partial_one), row_blocks(out_parts)
    one_a = send(parts[2], "seq", 1)
    one_b = send(outs[2], "seq", -1)
    n_attn = w_attn.shape[1]
    share_attn = scattered(grad_attn.reshape(RING, -1, grad_attn.shape[1]), 1)
    one_a, one_b, share_ff, *down_pieces = fence(one_a, one_b, share_ff, *down_pieces)
    after = jnp.concatenate([total(parts[1], one_a).astype(jnp.bfloat16), outs[1]], axis=0)
    before = jnp.concatenate([parts[3], total(outs[3], one_b).astype(jnp.bfloat16)], axis=0)
    from_last = send(after, "seq", 1)
    from_next = send(before, "seq", -1)
    ff_pieces = grp_pieces(share_ff.reshape(RING, RING, part, -1), 1)
    from_last, from_next, *ff_pieces = fence(from_last, from_next, *ff_pieces)
    ff_pieces = seq_pieces(total(*ff_pieces).astype(jnp.bfloat16))
    down_own = total(*down_pieces).astype(jnp.bfloat16)
    down_got = [send(down_own, "grp", -k) for k in range(1, RING)]
    down_got, ff_pieces = fence(down_got, ff_pieces)
    share_down = ordered([down_own] + down_got, grp_index).reshape(-1, width)
    share_down = share_down.astype(jnp.float32)
    ff_columns = by_source(ff_pieces, seq_index)
    ff_rows = jnp.concatenate(
        [side_by_side(ff_columns[:, :, :f_cols]), side_by_side(ff_columns[:, :, f_cols:])], axis=1
    )
    ff_after = send(ff_rows, "grp", -1)
    ff_before = send(ff_rows, "grp", 1)
    grad_normed_one = total(parts[0], from_last[:rows], from_next[:rows])
    result = middle + total(outs[0], from_last[rows:], from_next[rows:])
    layer_output = result.astype(jnp.bfloat16)[None, None]
    own_inputs = own_tokens.astype(jnp.float32)
    input_grad = grad_middle + norm_back(
        own_inputs, norm_scale(own_inputs), gain_one, grad_normed_one
    )
    ff_after, ff_before, input_grad, layer_output, share_attn = fence(
        ff_after, ff_before, input_grad, layer_output, share_attn
    )
    ff_far_a = send(ff_after[: part // 2], "grp", -1)
    ff_far_b = send(ff_before[part // 2 :], "grp", 1)
    pieces = grp_pieces(share_attn.reshape(RING, RING, part, -1), 1)
    ff_far_a, ff_far_b, ff_rows, *pieces = fence(ff_far_a, ff_far_b, ff_rows, *pieces)
    ff_far = jnp.concatenate([ff_far_a, ff_far_b], axis=0)
    ff_rows = ordered([ff_rows, ff_after, ff_far, ff_before], grp_index)
    ff_rows = ff_rows.reshape(own_rows, -1).astype(jnp.float32)
    share_gate = ff_rows[:, : RING * f_cols]
    share_upper = ff_rows[:, RING * f_cols :]
    summed = total(*pieces).astype(jnp.bfloat16)
    out_own = side_by_side(summed[:, :, n_attn:])
    columns = by_source(seq_pieces(summed[:, :, :n_attn]), seq_index)
    summed = total(*[columns[i, :, q_cols:] for i in range(RING)]).astype(jnp.bfloat16)
    attn_rows = jnp.concatenate(
        [side_by_side(columns[:, :, :q_cols]), out_own, summed], axis=1
    )
    attn_got = [send(attn_rows, "grp", -k) for k in range(1, RING)]
    attn_rows = ordered([attn_rows] + attn_got, grp_index).reshape(own_rows, -1)
    attn_rows = attn_rows.astype(jnp.float32)
    share_query = attn_rows[:, :width]
    share_out = attn_rows[:, width : 2 * width]
    share_pair = attn_rows[:, 2 * width : 2 * width + 2 * HD]
    share_gain_one = attn_rows[:, 2 * width + 2 * HD]
    share_gain_two = attn_rows[:, 2 * width + 2 * HD + 1]
    return (
        layer_output,
        input_grad[None, None],
        share_gain_one,
        share_query,
        share_pair,
        share_out,
        share_gain_two,
        share_gate,
        share_upper,
        share_down,
    )


def solution(mesh):
    by_row = P(("seq", "shard"), None)
    by_entry = P(("seq", "shard"))
    by_token = P("grp", "shard", "seq", None)
    return jax.shard_map(
        shards,
        mesh=mesh,
        in_specs=(
            by_token,
            P("grp", None),
            P("grp", None),
            by_entry,
            by_row,
            by_row,
            by_row,
            by_entry,
            by_row,
            by_row,
            by_row,
            by_token,
        ),
        out_specs=(
            by_token,
            by_token,
            by_entry,
            by_row,
            by_row,
            by_row,
            by_entry,
            by_row,
            by_row,
            by_row,
        ),
        check_vma=False,
    )
```
